256 devices in a mesh: dp: 8 (over z_lo, core), expert: 32 (over y, z_hi, x).
Axes of the slice: x: 4, y: 4, z: 8 (z_hi: 2, z_lo: 4; z = z_hi * 4 + z_lo), core: 2. Of those that a mesh axis runs over, the one named last changes fastest.
Arguments:
- tokens: bfloat16 [2, 1024, 7168], P(None, 'dp'), may hold values from -6 to 6
- scores: float32 [2, 1024, 8], P(None, 'dp'), may hold values from 0.05 to 1
- expert_ids: int32 [2, 1024, 8], P(None, 'dp'), may hold values from 0 to 31, all different within a row; in each aligned block of 128 rows (0 to 127, 128 to 255, ..., all dimensions but the last counted through in order) at most 48 rows name the same one
- slot_expert: int32 [32], replicated, may hold values from 0 to 31, each once
- w_gate: bfloat16 [32, 7168, 1024], P('expert', 'dp'), may hold values from -0.0625 to 0.0625
- w_up: bfloat16 [32, 7168, 1024], P('expert', 'dp'), may hold values from -0.0625 to 0.0625
- w_down: bfloat16 [32, 1024, 7168], P('expert', None, 'dp'), may hold values from -0.1875 to 0.1875
Outputs:
- mixed: bfloat16 [2, 1024, 7168], P(None, ('dp', 'expert'))
The draws below stay inside these ranges and needn't reach their ends.
Inputs may be any that keep to these rules, and one draw needn't show every extreme that they name: `expert_ids`: each token names 8 different experts. In each micro-batch the 128 tokens on one index of dp name any one expert at most 48 times; some of these blocks reach the bound. `slot_expert`: each expert stands in exactly one slot.
All inputs are finite; a program needn't handle non-finite values.
Results may differ from the reference program's by a relative error of at most 0.0058.
Values may be sent and summed in bfloat16 or wider, within the bound.
A program may use at most 64 MiB of HBM per device.

```python
import math
import jax
import jax.numpy as jnp
import numpy as np
from jax import lax

D = 7168
H = 1024
TOPK = 8
MB = 2
TOK_ROW = 128
EXPERTS = 32
TOKENS = 1024
CAP = 48
N_DP = 8


def shard_levels(own_key, shape, pieces, low, largest):
    def one(position, blocks):
        heights = jax.random.uniform(jax.random.fold_in(jax.random.fold_in(own_key, 6), position), (blocks,), jnp.float32, low / len(pieces), largest / len(pieces))
        return jnp.repeat(jnp.exp(heights), shape[position] // blocks).reshape((-1,) + (1,) * (len(shape) - position - 1))

    gain = one(*pieces[0])
    for cut in pieces[1:]:
        gain = gain * one(*cut)
    return gain


def assign_block(rng, own, number, rows, amount, top, limit, lean):
    sequence = jax.random.permutation(rng, amount)
    heavy_load, ordinary = portions_of(amount, rows * top, limit, lean, True), portions_of(amount, rows * top, limit, lean, False)
    places = jnp.arange(amount)

    def named(tallies, turn):
        used = int((tallies > 0).sum())
        fixed = max(1, used // 4)
        shifted = fixed + (places - fixed + turn * (used - fixed)) % max(1, amount - fixed)
        return jnp.zeros((amount,), jnp.int32).at[sequence[jnp.where(places < fixed, places, shifted)]].set(jnp.asarray(tallies, jnp.int32))

    tallies = jnp.where(number % 4 == 0, named(heavy_load, number // 4), named(ordinary, number - number // 4 - 1))
    mixed = jax.random.permutation(jax.random.fold_in(own, 3), amount)
    donor, receiver = mixed[0:amount // 2 * 2:2], mixed[1:amount // 2 * 2:2]
    slack = jnp.minimum(tallies[donor] - 1, limit - tallies[receiver]) // 2
    slack = jnp.where((donor == sequence[0]) | (receiver == sequence[0]) | (tallies[receiver] == 0), 0, jnp.maximum(slack, 0))
    shifted = jax.random.randint(jax.random.fold_in(own, 4), (amount // 2,), 0, 1 << 20) % (slack + 1)
    tallies = tallies.at[donor].add(-shifted).at[receiver].add(shifted)
    items = jnp.searchsorted(jnp.cumsum(tallies), jnp.arange(rows * top), side="right").astype(jnp.int32)
    listing = items.reshape(top, rows).T
    listing = listing[jax.random.permutation(jax.random.fold_in(own, 1), rows)]
    turn = jax.random.randint(jax.random.fold_in(own, 2), (rows, 1), 0, top)
    return jnp.take_along_axis(listing, (jnp.arange(top)[None, :] + turn) % top, axis=1)


def portions_of(count, total, limit, lean, full):
    weights = [(1 << 20) // math.isqrt(standing ** lean) + 1 for standing in range(1, count + 1)]
    largest = limit if full else min(limit, max(-(-total // count), total * weights[0] // sum(weights)))
    least = 1 if total - largest >= count - 1 else 0
    counts, surplus = [largest] + [least] * (count - 1), total - largest - least * (count - 1)
    while surplus > 0:
        candidates = [i for i in range(1, count) if counts[i] < largest] or [i for i in range(1, count) if counts[i] < limit]
        pool, left = sum([weights[i] for i in candidates]), surplus
        for i in candidates:
            extra = min(limit - counts[i], max(1, left * weights[i] // pool), surplus)
            counts[i] = counts[i] + extra
            surplus = surplus - extra
    return np.array(counts)


def centred(key, shape, scale, most, shards=(), dtype=jnp.bfloat16):
    gain = shard_levels(key, shape, shards, -0.22, 0.18) if shards else 1.0
    array = jax.random.normal(key, shape, jnp.float32) * scale * gain
    return jnp.minimum(jnp.maximum(array, -most), most).astype(dtype)


def setup_inputs(seed: int = 0) -> dict:
    seeds = jax.random.split(jax.random.key(seed), 8)
    tokens = centred(seeds[0], (MB, TOKENS, D), 1.0, 6.0, ((1, 8),))
    scores = jnp.clip(0.05 + 0.95 * jax.random.uniform(seeds[1], (MB, TOKENS, TOPK), jnp.float32) ** shard_levels(seeds[1], (MB, TOKENS, TOPK), ((1, 8),), -0.2, 0.2), 0.05, 1.0)
    expert_ids_keys = jax.random.split(jax.random.fold_in(seeds[2], 1), MB * TOKENS // TOK_ROW)
    expert_ids_turns = jax.random.permutation(jax.random.fold_in(seeds[2], 3), MB * TOKENS // TOK_ROW)
    expert_ids = jax.vmap(lambda own, number: assign_block(jax.random.fold_in(seeds[2], 2), own, number, TOK_ROW, EXPERTS, TOPK, CAP, 2))(expert_ids_keys, expert_ids_turns).reshape((MB, TOKENS, TOPK))
    slot_expert = jax.random.permutation(seeds[3], EXPERTS).astype(jnp.int32)
    w_gate = centred(seeds[4], (EXPERTS, D, H), D ** -0.5, 0.0625, ((0, 32), (1, 8)))
    w_up = centred(seeds[5], (EXPERTS, D, H), D ** -0.5, 0.0625, ((0, 32), (1, 8)))
    w_down = centred(seeds[6], (EXPERTS, H, D), H ** -0.5, 0.1875, ((0, 32), (2, 8)))
    return dict(tokens=tokens, scores=scores, expert_ids=expert_ids, slot_expert=slot_expert, w_gate=w_gate, w_up=w_up, w_down=w_down)


ROUTE_SCALE = 2.5


def reference(tokens, scores, expert_ids, slot_expert, w_gate, w_up, w_down):
    flat_tokens = tokens.reshape(MB * TOKENS, D)
    route_ids = expert_ids.reshape(MB * TOKENS, TOPK)
    raw_scores = scores.reshape(MB * TOKENS, TOPK).astype(jnp.float32)
    weights = ROUTE_SCALE * raw_scores / jnp.sum(raw_scores, axis=1, keepdims=True)
    row_limit = MB * N_DP * CAP

    def slot_step(totals, slot):
        expert_here = slot_expert[slot]
        matched = route_ids == expert_here
        shares = jnp.sum(jnp.where(matched, weights, jnp.float32(0.0)), axis=1)
        routed = jnp.any(matched, axis=1)
        picked = jnp.nonzero(routed, size=row_limit, fill_value=0)[0]
        chosen = flat_tokens[picked]
        gate_sum = jnp.dot(chosen, w_gate[slot], preferred_element_type=jnp.float32)
        up_sum = jnp.dot(chosen, w_up[slot], preferred_element_type=jnp.float32)
        hidden = (jax.nn.silu(gate_sum) * up_sum).astype(jnp.bfloat16)
        expert_out = jnp.dot(hidden, w_down[slot], preferred_element_type=jnp.float32).astype(jnp.bfloat16)
        filled = jnp.arange(row_limit).astype(jnp.int32) < jnp.sum(routed.astype(jnp.int32)).astype(jnp.int32)
        weighted = jnp.where(filled[:, None], shares[picked][:, None] * expert_out.astype(jnp.float32), jnp.float32(0.0))
        return totals.at[picked].add(weighted), None

    totals, _ = lax.scan(slot_step, jnp.zeros((MB * TOKENS, D), jnp.float32), jnp.arange(EXPERTS).astype(jnp.int32))
    return totals.reshape(MB, TOKENS, D).astype(jnp.bfloat16)
```

```python
import jax
import jax.numpy as jnp
from jax import lax
from jax.experimental import pallas as pl
from jax.experimental.pallas import tpu as pltpu
from jax.sharding import PartitionSpec as P

ROUTE_SCALE = 2.5
MESH = pl.DeviceIdType.MESH
F32 = jnp.float32
BF16 = jnp.bfloat16

MB = 2
ROWS = 128
CAP = 48
D = 7168
W = 896
H = 1024
HH = 512
NDP = 8
CH = 4


def div(a, b):
    return lax.div(a, jnp.int32(b))


def rem(a, b):
    return lax.rem(a, jnp.int32(b))


def kernel(
    tok_hbm, scores_ref, ids_ref, slot_ref, wg_hbm, wu_hbm, wd_hbm, out_ref,
    tok, wgu, wd, pick, pk, xin, part, bsend, brecv, hid, yv, zf, e1s, e1r, tf, e2s, e2r, uv,
    fs, fr, rts, rtr,
    s_loc, s_w, r_w, s_rt, r_rt, s_a, r_a, s_f, r_f, s_o, r_o,
    s_b, r_b, s_c, r_c, s_p, r_p, s_e1, r_e1, s_e2, r_e2, s_x, r_x,
):
    dp = lax.axis_index("dp")
    ex = lax.axis_index("expert")
    zl, c = div(dp, 2), rem(dp, 2)
    y, zh, x = div(ex, 8), rem(div(ex, 4), 2), rem(ex, 4)
    z = zh * 4 + zl
    oc = 1 - c
    peer = (zl * 2 + oc, ex)

    def column(zz, cc):
        return (rem(zz, 4) * 2 + cc, (y * 2 + div(zz, 4)) * 4 + x)

    def xdev(xx):
        return (dp, (y * 2 + zh) * 4 + xx)

    def ydev(yy):
        return (dp, (yy * 2 + zh) * 4 + x)

    def remote(src, dst, ssem, rsem, dev):
        return pltpu.make_async_remote_copy(
            src_ref=src, dst_ref=dst, send_sem=ssem, recv_sem=rsem,
            device_id=dev, device_id_type=MESH,
        )

    bar = pltpu.get_barrier_semaphore()
    for a in range(NDP):
        for b in range(2):
            if a or b:
                dev = (rem(dp + a, NDP), (y * 2 + rem(zh + b, 2)) * 4 + x)
                pl.semaphore_signal(bar, inc=1, device_id=dev, device_id_type=MESH)
    for a in range(1, 4):
        pl.semaphore_signal(bar, inc=1, device_id=xdev(rem(x + a, 4)), device_id_type=MESH)
        pl.semaphore_signal(bar, inc=1, device_id=ydev(rem(y + a, 4)), device_id_type=MESH)

    mine = pl.ds(pl.multiple_of(c * HH, 128), HH)
    theirs = pl.ds(pl.multiple_of(oc * HH, 128), HH)
    loads = [
        pltpu.make_async_copy(tok_hbm.at[0], tok.at[0], s_loc.at[0]),
        pltpu.make_async_copy(tok_hbm.at[1], tok.at[1], s_loc.at[1]),
        pltpu.make_async_copy(wg_hbm.at[0, :, mine], wgu.at[c, :, pl.ds(0, HH)], s_loc.at[2]),
        pltpu.make_async_copy(wu_hbm.at[0, :, mine], wgu.at[c, :, pl.ds(HH, HH)], s_loc.at[3]),
        pltpu.make_async_copy(wd_hbm.at[0], wd, s_loc.at[4]),
    ]
    for cp in loads:
        cp.start()

    lane = lax.broadcasted_iota(jnp.int32, (ROWS, 128), 1)
    sub = lax.broadcasted_iota(jnp.int32, (ROWS, 128), 0)
    cols = jnp.zeros((ROWS, 128), F32)
    for mb in range(MB):
        sc = scores_ref[mb]
        ids = ids_ref[mb]
        wts = ROUTE_SCALE * sc / jnp.sum(sc, axis=1, keepdims=True)
        for zz in range(2):
            logical = slot_ref[(y * 2 + zz) * 4 + x]
            hit = ids == logical
            share = jnp.sum(jnp.where(hit, wts, 0.0), axis=1, keepdims=True)
            there = jnp.sum(jnp.where(hit, 1.0, 0.0), axis=1, keepdims=True)
            cols = cols + jnp.where(lane == zz * 4 + mb, there, 0.0)
            cols = cols + jnp.where(lane == zz * 4 + 2 + mb, share, 0.0)
    rows = jnp.transpose(cols)[0:8]
    before = jnp.where(sub < lane, 1.0, 0.0).astype(BF16)
    ranks = jnp.dot(rows.astype(BF16), before, preferred_element_type=F32)
    ranks = jnp.where(rows > 0.0, ranks, -1.0)
    row8 = lax.broadcasted_iota(jnp.int32, (8, 128), 0)
    info = jnp.where(rem(row8, 4) < 2, ranks, rows)
    place = lax.broadcasted_iota(jnp.int32, (CAP, 128), 0).astype(F32)
    for zz in range(2):
        for mb in range(MB):
            r = zz * 4 + mb
            pick[zz, mb] = jnp.where(place == ranks[r : r + 1], 1.0, 0.0).astype(BF16)
    hi, mid = div(lane, 32), rem(div(lane, 8), 4)
    xx = jnp.where(dp < 4, hi, mid)
    yy = jnp.where(dp < 4, mid, hi)
    home = yy * 32 + rem(div(lane, 4), 2) * 16 + xx * 4 + rem(lane, 4)
    order = jnp.where(sub == home, 1.0, 0.0)
    info = jnp.dot(info, order, preferred_element_type=F32, precision=lax.Precision.HIGHEST)
    rts[...] = info
    rtr[dp] = info

    two = jnp.where(c == 1, z + 2, z + 6)
    dest_z = [rem(two, 8)] * 2 + [rem(z + 1, 8)] * 2 + [rem(z + 7, 8)] * 2
    from_z = [rem(zl + 2, 4)] * 2 + [rem(zl + 1, 4)] * 2 + [rem(zl + 3, 4)] * 2
    source = [from_z[n] * 2 + n % 2 for n in range(6)]

    def pack(mb, zz, j):
        piece = tok[mb, :, pl.ds(pl.multiple_of(j * W, 128), W)]
        return jnp.dot(pick[zz, mb], piece, preferred_element_type=F32).astype(BF16)

    def piece_copy(mb, n):
        return remote(
            pk.at[mb, n], xin.at[mb, n % 2, dp], s_a.at[mb, n], r_a.at[mb, dp],
            column(dest_z[n], n % 2),
        )

    def forward_copy(mb, n):
        i = source[n]
        return remote(xin.at[mb, c, i], xin.at[mb, c, i], s_f.at[mb, n], r_f.at[mb, i], peer)

    def own_copy(mb):
        return remote(xin.at[mb, :, dp], xin.at[mb, :, dp], s_o.at[mb], r_o.at[mb], peer)

    def weight_copies():
        return [
            remote(
                wg_hbm.at[0, :, theirs], wgu.at[c, :, pl.ds(0, HH)], s_w.at[0], r_w.at[0], peer
            ),
            remote(
                wu_hbm.at[0, :, theirs], wgu.at[c, :, pl.ds(HH, HH)], s_w.at[1], r_w.at[1], peer
            ),
        ]

    def info_copies():
        out = [
            remote(rts, rtr.at[dp], s_rt.at[n], r_rt.at[dp], column(dest_z[n], n % 2))
            for n in range(6)
        ]
        return out + [remote(rts, rtr.at[dp], s_rt.at[6], r_rt.at[dp], peer)]

    def dispatch(mb):
        for n in range(6):
            pk[mb, n] = pack(mb, div(dest_z[n], 4), rem(dest_z[n], 4) * 2 + n % 2)
            if mb == 0 and n == 0:
                pl.semaphore_wait(bar, 21)
            piece_copy(mb, n).start()
        for k in range(2):
            xin[mb, k, dp] = pack(mb, zh, zl * 2 + k)
        own_copy(mb).start()

    def collect(mb):
        for n in (2, 3, 4, 5, 0, 1):
            i = source[n]
            remote(
                pk.at[mb, n], xin.at[mb, c, i], s_a.at[mb, n], r_a.at[mb, i], peer
            ).wait_recv()
            forward_copy(mb, n).start()
        own = remote(
            xin.at[mb, :, dp], xin.at[mb, :, zl * 2 + oc], s_o.at[mb], r_o.at[mb], peer
        )
        own.wait_recv()
        for n in (2, 3, 4, 5, 0, 1):
            i = source[n]
            remote(
                xin.at[mb, c, i], xin.at[mb, oc, i], s_f.at[mb, n], r_f.at[mb, i], peer
            ).wait_recv()

    def project_in(mb):
        @pl.loop(0, 4)
        def _(nb):
            at = pl.ds(pl.multiple_of(nb * 256, 128), 256)
            total = jnp.dot(
                xin[mb, 0].reshape(NDP * CAP, W), wgu[0, :, at], preferred_element_type=F32
            ) + jnp.dot(
                xin[mb, 1].reshape(NDP * CAP, W), wgu[1, :, at], preferred_element_type=F32
            )
            part[mb, :, :, at] = total.reshape(NDP, CAP, 256)

    def chain(d, k):
        mb, i = div(k, CH), rem(k, CH) + 4 * (1 - d)
        p = zl if d == 0 else 3 - zl
        up = (dp + 2 if d == 0 else dp - 2, ex)
        down = (dp - 2 if d == 0 else dp + 2, ex)
        slot = hid.at[mb, c, i]
        sums = remote(bsend.at[d, k], brecv.at[d, k], s_b.at[d, k], r_b.at[d, k], up)
        relay = remote(slot, slot, s_c.at[d, k], r_c.at[d, k], down)
        across = remote(slot, slot, s_p.at[d, k], r_p.at[d, k], peer)
        return mb, i, p, sums, relay, across

    def chain_step(t):
        for d in range(2):
            p0 = zl if d == 0 else 3 - zl
            k = t - p0

            @pl.when((k >= 0) & (k < MB * CH))
            def _():
                mb, i, p, sums, relay, across = chain(d, k)

                @pl.when(p == 0)
                def _():
                    bsend[d, k] = part[mb, i].astype(BF16)

                @pl.when(p > 0)
                def _():
                    sums.wait_recv()

                @pl.when((p > 0) & (p < 3))
                def _():
                    bsend[d, k] = (part[mb, i] + brecv[d, k].astype(F32)).astype(BF16)

                @pl.when(p < 3)
                def _():
                    sums.start()

                @pl.when(p == 3)
                def _():
                    gate = part[mb, i, :, 0:HH] + brecv[d, k, :, 0:HH].astype(F32)
                    lift = part[mb, i, :, HH:H] + brecv[d, k, :, HH:H].astype(F32)
                    hid[mb, c, i] = (gate / (1.0 + jnp.exp(-gate)) * lift).astype(BF16)
                    relay.start()
                    across.start()

            k2 = t - 6 + p0

            @pl.when((p0 < 3) & (k2 >= 0) & (k2 < MB * CH))
            def _():
                mb, i, p, sums, relay, across = chain(d, k2)
                relay.wait_recv()

                @pl.when(p > 0)
                def _():
                    relay.start()

                across.start()

    def chain_sends():
        @pl.loop(0, MB * CH)
        def _(k):
            for d in range(2):
                mb, i, p, sums, relay, across = chain(d, k)

                @pl.when(p < 3)
                def _():
                    sums.wait_send()

                @pl.when(p > 0)
                def _():
                    relay.wait_send()

                across.wait_send()

    def project_out(mb):
        for d in range(2):
            for q in range(CH):
                i = q + 4 * (1 - d)
                remote(
                    hid.at[mb, c, i], hid.at[mb, oc, i],
                    s_p.at[d, mb * CH + q], r_p.at[d, mb * CH + q], peer,
                ).wait_recv()
        rows_out = jnp.dot(
            hid[mb, 0].reshape(NDP * CAP, HH), wd[0:HH], preferred_element_type=F32
        ) + jnp.dot(hid[mb, 1].reshape(NDP * CAP, HH), wd[HH:H], preferred_element_type=F32)
        yv[...] = rows_out.astype(BF16).reshape(NDP, CAP, W)

    def e1_copy(mb, g, a):
        to = rem((x if g == 0 else y) + a, 4)
        dev = xdev(to) if g == 0 else ydev(to)
        return remote(
            e1s.at[mb, g, to], e1r.at[mb, g, a - 1], s_e1.at[mb, g, a - 1],
            r_e1.at[mb, g, a - 1], dev,
        )

    def e2_copy(mb, g, a):
        to = rem((y if g == 0 else x) + a, 4)
        dev = ydev(to) if g == 0 else xdev(to)
        return remote(
            e2s.at[mb, g, to], e2r.at[mb, g, a - 1], s_e2.at[mb, g, a - 1],
            r_e2.at[mb, g, a - 1], dev,
        )

    def spread(mb):
        spot = lax.broadcasted_iota(jnp.int32, (ROWS, CAP), 1).astype(F32)
        for g in range(2):
            for ii in range(4):
                turned = jnp.transpose(rtr[g * 4 + ii])
                rank = jnp.where(zh == 0, turned[:, mb : mb + 1], turned[:, 4 + mb : 5 + mb])
                share = jnp.where(
                    zh == 0, turned[:, 2 + mb : 3 + mb], turned[:, 6 + mb : 7 + mb]
                )
                one = jnp.where(rank == spot, 1.0, 0.0).astype(BF16)
                value = share * jnp.dot(one, yv[g * 4 + ii], preferred_element_type=F32)
                value = value.reshape(4, 32, W)
                zf[g, :, ii] = value
                e1s[mb, g, :, ii] = value.astype(BF16)
            for a in (2, 1, 3):
                e1_copy(mb, g, a).start()

    def combine1(mb):
        for g in range(2):
            for a in (1, 3, 2):
                e1_copy(mb, g, a).wait_recv()
            own = x if g == 0 else y
            for ii in range(4):
                total = zf[g, own, ii]
                for a in range(3):
                    total = total + e1r[mb, g, a, ii].astype(F32)
                tf[g, :, ii] = total.reshape(4, 8, W)
            for b in range(4):
                e2s[mb, g, b] = tf[g, b].reshape(32, W).astype(BF16)
            for a in (2, 1, 3):
                e2_copy(mb, g, a).start()

    def combine2(mb):
        for g in range(2):
            for a in (1, 3, 2):
                e2_copy(mb, g, a).wait_recv()
            own = y if g == 0 else x
            total = tf[g, own].reshape(32, W)
            for a in range(3):
                total = total + e2r[mb, g, a].astype(F32)
            uv[mb, g] = total.reshape(4, 8, W)

    def deliver_copy(a, b):
        i, zz = rem(dp + a, NDP), rem(zh + b, 2)
        dev = (i, (y * 2 + zz) * 4 + x)
        n = a * 2 + b
        return remote(fs.at[n], fr.at[dp, zh], s_x.at[n], r_x.at[dp, zh], dev)

    def deliver():
        top = lax.broadcasted_iota(jnp.int32, (8, W), 0) < 4
        for a in (4, 3, 5, 2, 6, 1, 7, 0):
            i = rem(dp + a, NDP)
            u0, u1 = uv[0, div(i, 4), rem(i, 4)], uv[1, div(i, 4), rem(i, 4)]
            first = jnp.where(top, u0, pltpu.roll(u1, 4, 0))
            second = jnp.where(top, pltpu.roll(u0, 4, 0), u1)
            same = jnp.where(zh == 0, first, second)
            other = jnp.where(zh == 0, second, first)
            fs[a * 2 + 1] = other
            deliver_copy(a, 1).start()
            if a:
                fs[a * 2] = same
                deliver_copy(a, 0).start()
            else:
                fr[dp, zh] = same
        for a in range(NDP):
            for b in range(2):
                if a or b:
                    j, zz = rem(dp + NDP - a, NDP), rem(zh + b, 2)
                    remote(
                        fs.at[a * 2 + b], fr.at[j, zz], s_x.at[a * 2 + b], r_x.at[j, zz], peer
                    ).wait_recv()
        for j in range(NDP):
            out_ref[:, j * W : (j + 1) * W] = (fr[j, 0] + fr[j, 1]).astype(BF16)

    loads[0].wait()
    dispatch(0)
    for cp in weight_copies():
        cp.start()
    for cp in info_copies():
        cp.start()
    loads[1].wait()
    dispatch(1)
    loads[2].wait()
    loads[3].wait()
    for k in range(2):
        at = pl.ds(k * HH, HH)
        remote(
            wg_hbm.at[0, :, theirs], wgu.at[oc, :, at], s_w.at[k], r_w.at[k], peer
        ).wait_recv()
    collect(0)
    project_in(0)

    @pl.loop(0, CH)
    def _(t):
        chain_step(t)

    collect(1)
    project_in(1)

    @pl.loop(CH, CH + 6)
    def _(t):
        chain_step(t)

    loads[4].wait()
    for n in range(6):
        remote(rts, rtr.at[source[n]], s_rt.at[n], r_rt.at[source[n]], peer).wait_recv()
    remote(rts, rtr.at[zl * 2 + oc], s_rt.at[6], r_rt.at[zl * 2 + oc], peer).wait_recv()
    project_out(0)
    spread(0)

    @pl.loop(CH + 6, 2 * CH + 6)
    def _(t):
        chain_step(t)

    combine1(0)
    project_out(1)
    spread(1)
    combine2(0)
    combine1(1)
    combine2(1)
    deliver()

    for cp in weight_copies() + info_copies():
        cp.wait_send()
    chain_sends()
    for mb in range(MB):
        own_copy(mb).wait_send()
        for n in range(6):
            piece_copy(mb, n).wait_send()
            forward_copy(mb, n).wait_send()
        for g in range(2):
            for a in range(1, 4):
                e1_copy(mb, g, a).wait_send()
                e2_copy(mb, g, a).wait_send()
    for a in range(NDP):
        for b in range(2):
            if a or b:
                deliver_copy(a, b).wait_send()


def per_device(tokens, scores, expert_ids, slot_expert, w_gate, w_up, w_down):
    vmem = pl.BlockSpec(memory_space=pltpu.VMEM)
    anywhere = pl.BlockSpec(memory_space=pl.ANY)
    dma = pltpu.SemaphoreType.DMA
    out = pl.pallas_call(
        kernel,
        out_shape=jax.ShapeDtypeStruct((8, D), BF16),
        in_specs=[
            anywhere, vmem, vmem, pl.BlockSpec(memory_space=pltpu.SMEM),
            anywhere, anywhere, anywhere,
        ],
        out_specs=vmem,
        scratch_shapes=[
            pltpu.VMEM((MB, ROWS, D), BF16),
            pltpu.VMEM((2, W, H), BF16),
            pltpu.VMEM((H, W), BF16),
            pltpu.VMEM((2, MB, CAP, 128), BF16),
            pltpu.VMEM((MB, 6, CAP, W), BF16),
            pltpu.VMEM((MB, 2, NDP, CAP, W), BF16),
            pltpu.VMEM((MB, NDP, CAP, H), F32),
            pltpu.VMEM((2, MB * CH, CAP, H), BF16),
            pltpu.VMEM((2, MB * CH, CAP, H), BF16),
            pltpu.VMEM((MB, 2, NDP, CAP, HH), BF16),
            pltpu.VMEM((NDP, CAP, W), BF16),
            pltpu.VMEM((2, 4, 4, 32, W), F32),
            pltpu.VMEM((MB, 2, 4, 4, 32, W), BF16),
            pltpu.VMEM((MB, 2, 3, 4, 32, W), BF16),
            pltpu.VMEM((2, 4, 4, 8, W), F32),
            pltpu.VMEM((MB, 2, 4, 32, W), BF16),
            pltpu.VMEM((MB, 2, 3, 32, W), BF16),
            pltpu.VMEM((MB, 2, 4, 8, W), F32),
            pltpu.VMEM((16, 8, W), F32),
            pltpu.VMEM((NDP, 2, 8, W), F32),
            pltpu.VMEM((8, 128), F32),
            pltpu.VMEM((NDP, 8, 128), F32),
            dma((5,)),
            dma((2,)), dma((2,)),
            dma((7,)), dma((NDP,)),
            dma((MB, 6)), dma((MB, NDP)),
            dma((MB, 6)), dma((MB, NDP)),
            dma((MB,)), dma((MB,)),
            dma((2, MB * CH)), dma((2, MB * CH)),
            dma((2, MB * CH)), dma((2, MB * CH)),
            dma((2, MB * CH)), dma((2, MB * CH)),
            dma((MB, 2, 3)), dma((MB, 2, 3)),
            dma((MB, 2, 3)), dma((MB, 2, 3)),
            dma((16,)), dma((NDP, 2)),
        ],
        compiler_params=pltpu.CompilerParams(
            collective_id=0, has_side_effects=True, vmem_limit_bytes=56 * 2**20
        ),
        name="expert_layer",
    )(tokens, scores, expert_ids, slot_expert, w_gate, w_up, w_down)
    return out.reshape(MB, 4, D)


def solution(mesh):
    in_specs = (
        P(None, "dp", None),
        P(None, "dp", None),
        P(None, "dp", None),
        P(),
        P("expert", "dp", None),
        P("expert", "dp", None),
        P("expert", None, "dp"),
    )
    out_specs = P(None, ("dp", "expert"), None)
    return jax.shard_map(
        per_device, mesh=mesh, in_specs=in_specs, out_specs=out_specs, check_vma=False
    )
```

```python
import jax
import jax.numpy as jnp
from jax import lax
from jax.experimental import pallas as pl
from jax.experimental.pallas import tpu as pltpu
from jax.sharding import PartitionSpec as P

ROUTE_SCALE = 2.5
MESH = pl.DeviceIdType.MESH
F32 = jnp.float32
BF16 = jnp.bfloat16

MB = 2
ROWS = 128
CAP = 48
D = 7168
W = 896
H = 1024
HH = 512
NDP = 8
HQ = 256
NCH = 16
UNITS = 8
WF = 512
SKEW = 3
PIECES = 16
LAG0 = 6 * SKEW + 2
LAG1 = LAG0 + 6
LAG2 = LAG1 + 6
LAG3 = LAG2 + 6


def div(a, b):
    return lax.div(a, jnp.int32(b))


def rem(a, b):
    return lax.rem(a, jnp.int32(b))


def kernel(
    tok_hbm, scores_ref, ids_ref, slot_ref, wg_hbm, wu_hbm, wd_hbm, out_ref,
    tok, wgu, wd, pick, pk, xin, part, bsend, brecv, hid, zf, zown, keep, e1s, e1r, m1s, m1r, e2s, e2r,
    fs, fr, rts, rtr,
    s_loc, s_w, r_w, s_rt, r_rt, s_a, r_a, s_f, r_f, s_o, r_o,
    s_b, r_b, s_c, r_c, s_p, r_p, s_e1, r_e1, s_m1, r_m1, s_e2, r_e2, s_x, r_x,
):
    dp = lax.axis_index("dp")
    ex = lax.axis_index("expert")
    zl, c = div(dp, 2), rem(dp, 2)
    y, zh, x = div(ex, 8), rem(div(ex, 4), 2), rem(ex, 4)
    z = zh * 4 + zl
    oc = 1 - c
    peer = (zl * 2 + oc, ex)

    def column(zz, cc):
        return (rem(zz, 4) * 2 + cc, (y * 2 + div(zz, 4)) * 4 + x)

    def xdev(xx):
        return (dp, (y * 2 + zh) * 4 + xx)

    def ydev(yy):
        return (dp, (yy * 2 + zh) * 4 + x)

    def remote(src, dst, ssem, rsem, dev):
        return pltpu.make_async_remote_copy(
            src_ref=src, dst_ref=dst, send_sem=ssem, recv_sem=rsem,
            device_id=dev, device_id_type=MESH,
        )

    bar = pltpu.get_barrier_semaphore()
    for a in range(NDP):
        for b in range(2):
            if a or b:
                dev = (rem(dp + a, NDP), (y * 2 + rem(zh + b, 2)) * 4 + x)
                pl.semaphore_signal(bar, inc=1, device_id=dev, device_id_type=MESH)
    for a in range(1, 4):
        pl.semaphore_signal(bar, inc=1, device_id=xdev(rem(x + a, 4)), device_id_type=MESH)
        pl.semaphore_signal(bar, inc=1, device_id=ydev(rem(y + a, 4)), device_id_type=MESH)

    def hidden_at(core, half):
        return pl.ds(pl.multiple_of(core * HH + half * HQ, 128), HQ)

    def weight_at(k):
        return (wg_hbm, wu_hbm)[k % 2], pl.ds(k * HQ, HQ)

    loads = [pltpu.make_async_copy(tok_hbm.at[mb], tok.at[mb], s_loc.at[mb]) for mb in range(MB)]
    for k in range(4):
        ref, at = weight_at(k)
        loads.append(
            pltpu.make_async_copy(
                ref.at[0, :, hidden_at(c, k // 2)], wgu.at[c, :, at], s_loc.at[2 + k]
            )
        )
    loads.append(pltpu.make_async_copy(wd_hbm.at[0], wd, s_loc.at[6]))
    for cp in loads:
        cp.start()

    row8 = lax.broadcasted_iota(jnp.int32, (8, ROWS), 0)
    rows = jnp.zeros((8, ROWS), F32)
    for mb in range(MB):
        sc = scores_ref[mb]
        ids = ids_ref[mb]
        wts = ROUTE_SCALE * sc / jnp.sum(sc, axis=0, keepdims=True)
        for zz in range(2):
            logical = slot_ref[(y * 2 + zz) * 4 + x]
            hit = ids == logical
            share = jnp.sum(jnp.where(hit, wts, 0.0), axis=0, keepdims=True)
            there = jnp.sum(jnp.where(hit, 1.0, 0.0), axis=0, keepdims=True)
            rows = jnp.where(row8 == zz * 4 + mb, there, rows)
            rows = jnp.where(row8 == zz * 4 + 2 + mb, share, rows)
    lane = lax.broadcasted_iota(jnp.int32, (ROWS, ROWS), 1)
    sub = lax.broadcasted_iota(jnp.int32, (ROWS, ROWS), 0)
    before = jnp.where(sub < lane, 1.0, 0.0).astype(BF16)
    ranks = jnp.dot(rows.astype(BF16), before, preferred_element_type=F32)
    ranks = jnp.where(rows > 0.0, ranks, -1.0)
    info = jnp.where(rem(row8, 4) < 2, ranks, rows)
    place = lax.broadcasted_iota(jnp.int32, (CAP, ROWS), 0).astype(F32)
    for zz in range(2):
        for mb in range(MB):
            r = zz * 4 + mb
            pick[zz, mb] = jnp.where(place == ranks[r : r + 1], 1.0, 0.0).astype(BF16)

    two = jnp.where(c == 1, z + 2, z + 6)
    dest_z = [rem(two, 8)] * 2 + [rem(z + 1, 8)] * 2 + [rem(z + 7, 8)] * 2
    from_z = [rem(zl + 2, 4)] * 2 + [rem(zl + 1, 4)] * 2 + [rem(zl + 3, 4)] * 2
    source = [from_z[n] * 2 + n % 2 for n in range(6)]

    def pack(mb, zz, j):
        piece = tok[mb, :, pl.ds(pl.multiple_of(j * W, 128), W)]
        return jnp.dot(pick[zz, mb], piece, preferred_element_type=F32).astype(BF16)

    def piece_copy(mb, n):
        return remote(
            pk.at[mb, n], xin.at[mb, n % 2, dp], s_a.at[mb, n], r_a.at[mb, dp],
            column(dest_z[n], n % 2),
        )

    def forward_copy(mb, n):
        i = source[n]
        return remote(xin.at[mb, c, i], xin.at[mb, c, i], s_f.at[mb, n], r_f.at[mb, i], peer)

    def own_copy(mb):
        return remote(xin.at[mb, :, dp], xin.at[mb, :, dp], s_o.at[mb], r_o.at[mb], peer)

    def weight_copies():
        out = []
        for k in range(4):
            ref, at = weight_at(k)
            out.append(
                remote(
                    ref.at[0, :, hidden_at(oc, k // 2)], wgu.at[c, :, at],
                    s_w.at[k], r_w.at[k], peer,
                )
            )
        return out

    def info_copies():
        out = [
            remote(rts, rtr.at[dp], s_rt.at[n], r_rt.at[dp], column(dest_z[n], n % 2))
            for n in range(6)
        ]
        return out + [remote(rts, rtr.at[dp], s_rt.at[6], r_rt.at[dp], peer)]

    def dispatch(mb):
        for n in range(6):
            pk[mb, n] = pack(mb, div(dest_z[n], 4), rem(dest_z[n], 4) * 2 + n % 2)
            if mb == 0 and n == 0:
                pl.semaphore_wait(bar, 21)
            piece_copy(mb, n).start()
        for k in range(2):
            xin[mb, k, dp] = pack(mb, zh, zl * 2 + k)
        own_copy(mb).start()

    def announce():
        hi, mid = div(lane, 32), rem(div(lane, 8), 4)
        xx = jnp.where(dp < 4, hi, mid)
        yy = jnp.where(dp < 4, mid, hi)
        home = yy * 32 + rem(div(lane, 4), 2) * 16 + xx * 4 + rem(lane, 4)
        order = jnp.where(sub == home, 1.0, 0.0)
        told = jnp.dot(info, order, preferred_element_type=F32, precision=lax.Precision.HIGHEST)
        rts[...] = told
        rtr[dp] = told
        for cp in info_copies():
            cp.start()

    def collect(mb):
        for n in (2, 3, 4, 5, 0, 1):
            i = source[n]
            remote(
                pk.at[mb, n], xin.at[mb, c, i], s_a.at[mb, n], r_a.at[mb, i], peer
            ).wait_recv()
            forward_copy(mb, n).start()
        own = remote(
            xin.at[mb, :, dp], xin.at[mb, :, zl * 2 + oc], s_o.at[mb], r_o.at[mb], peer
        )
        own.wait_recv()
        for n in (2, 3, 4, 5, 0, 1):
            i = source[n]
            remote(
                xin.at[mb, c, i], xin.at[mb, oc, i], s_f.at[mb, n], r_f.at[mb, i], peer
            ).wait_recv()

    def project_in(mb, n):
        at = pl.ds(n * HQ, HQ)
        total = jnp.dot(
            xin[mb, 0].reshape(NDP * CAP, W), wgu[0, :, at], preferred_element_type=F32
        ) + jnp.dot(
            xin[mb, 1].reshape(NDP * CAP, W), wgu[1, :, at], preferred_element_type=F32
        )
        part[mb, :, n // 2, :, (n % 2) * HQ : (n % 2 + 1) * HQ] = total.reshape(NDP, CAP, HQ)

    def chain(d, k):
        half, u = rem(k, 2), div(k, 2)
        q, mb = rem(u, 4), div(u, 4)
        p = zl if d == 0 else 3 - zl
        up = (dp + 2 if d == 0 else dp - 2, ex)
        down = (dp - 2 if d == 0 else dp + 2, ex)
        slot = hid.at[u, c, half, 1 - d]
        own = part.at[mb, q + 4 * (1 - d), half]
        sums = remote(bsend.at[d, k], brecv.at[d, k], s_b.at[d, k], r_b.at[d, k], up)
        relay = remote(slot, slot, s_c.at[d, k], r_c.at[d, k], down)
        across = remote(slot, slot, s_p.at[d, k], r_p.at[d, k], peer)
        return own, slot, p, sums, relay, across

    def chain_step(t):
        for d in range(2):
            p0 = zl if d == 0 else 3 - zl
            k = t - SKEW * p0

            @pl.when((k >= 0) & (k < NCH))
            def _():
                own, slot, p, sums, relay, across = chain(d, k)

                @pl.when(p == 0)
                def _():
                    bsend[d, k] = own[...].astype(BF16)

                @pl.when(p > 0)
                def _():
                    sums.wait_recv()

                @pl.when((p > 0) & (p < 3))
                def _():
                    bsend[d, k] = (own[...] + brecv[d, k].astype(F32)).astype(BF16)

                @pl.when(p < 3)
                def _():
                    sums.start()

                @pl.when(p == 3)
                def _():
                    gate = own[:, 0:HQ] + brecv[d, k, :, 0:HQ].astype(F32)
                    lift = own[:, HQ : 2 * HQ] + brecv[d, k, :, HQ : 2 * HQ].astype(F32)
                    slot[...] = (gate / (1.0 + jnp.exp(-gate)) * lift).astype(BF16)
                    relay.start()
                    across.start()

        for d in range(2):
            p0 = zl if d == 0 else 3 - zl
            k2 = t - SKEW * (6 - p0)

            @pl.when((p0 < 3) & (k2 >= 0) & (k2 < NCH))
            def _():
                own, slot, p, sums, relay, across = chain(d, k2)
                relay.wait_recv()

                @pl.when(p > 0)
                def _():
                    relay.start()

                across.start()

    def chain_sends():
        @pl.loop(0, NCH)
        def _(k):
            for d in range(2):
                own, slot, p, sums, relay, across = chain(d, k)

                @pl.when(p < 3)
                def _():
                    sums.wait_send()

                @pl.when(p > 0)
                def _():
                    relay.wait_send()

                across.wait_send()

    def split(w):
        u, g = div(w, 2), rem(w, 2)
        return u, g, div(u, 4), rem(u, 4)

    def project_out(w):
        u, g, mb, q = split(w)
        for half in range(2):
            there = hid.at[u, oc, half, g]
            k = u * 2 + half
            remote(there, there, s_p.at[1 - g, k], r_p.at[1 - g, k], peer).wait_recv()
        total = jnp.zeros((CAP, W), F32)
        for core in range(2):
            for half in range(2):
                total = total + jnp.dot(
                    hid[u, core, half, g],
                    wd[core * HH + half * HQ : core * HH + (half + 1) * HQ],
                    preferred_element_type=F32,
                )
        return total.astype(BF16)

    def expert_at(g, a, first):
        along_x = (g == 0) == first
        to_x = jnp.where(along_x, rem(x + a, 4), x)
        to_y = jnp.where(along_x, y, rem(y + a, 4))
        return (dp, (to_y * 2 + zh) * 4 + to_x)

    def e1_copy(w, d):
        dev = expert_at(rem(w, 2), 1 if d == 0 else 3, True)
        return remote(e1s.at[w, d], e1r.at[w, d], s_e1.at[w, d], r_e1.at[w, d], dev)

    def m1_copy(w, d):
        dev = expert_at(rem(w, 2), 1 if d == 0 else 3, True)
        return remote(m1s.at[w, d], m1r.at[w, d], s_m1.at[w, d], r_m1.at[w, d], dev)

    def e2_copy(w, a):
        g = rem(w, 2)
        to = rem(jnp.where(g == 0, y, x) + a, 4)
        dev = expert_at(g, a, False)
        return remote(
            e2s.at[w, to], e2r.at[w, a - 1], s_e2.at[w, a - 1], r_e2.at[w, a - 1], dev
        )

    def spread(w):
        u, g, mb, q = split(w)
        rows_out = project_out(w)
        spot = lax.broadcasted_iota(jnp.int32, (ROWS, CAP), 1).astype(F32)
        row = lax.broadcasted_iota(jnp.int32, (8, ROWS), 0)
        told = rtr[g * 4 + q]
        rank = jnp.sum(jnp.where(row == zh * 4 + mb, told, 0.0), axis=0, keepdims=True)
        share = jnp.sum(jnp.where(row == zh * 4 + 2 + mb, told, 0.0), axis=0, keepdims=True)
        turned = jnp.transpose(jnp.where(row == 0, rank, share))
        one = jnp.where(turned[:, 0:1] == spot, 1.0, 0.0).astype(BF16)
        value = turned[:, 1:2] * jnp.dot(one, rows_out, preferred_element_type=F32)
        zf[...] = value.reshape(4, 32, W)
        at = jnp.where(g == 0, x, y)
        above, far, below = rem(at + 1, 4), rem(at + 2, 4), rem(at + 3, 4)
        e1s[w, 0, 0:16] = zf[far, 0:16].astype(BF16)
        e1s[w, 0, 16:32] = zf[above, 16:32].astype(BF16)
        e1s[w, 1, 0:16] = zf[far, 16:32].astype(BF16)
        e1s[w, 1, 16:32] = zf[below, 0:16].astype(BF16)
        for d in range(2):
            e1_copy(w, d).start()
        keep[w, 0] = zf[above, 0:16]
        keep[w, 1] = zf[below, 16:32]
        zown[w] = zf[at]

    def merge(w):
        for d in range(2):
            e1_copy(w, d).wait_recv()
            m1s[w, d] = (keep[w, d] + e1r[w, d, 0:16].astype(F32)).astype(BF16)
            m1_copy(w, d).start()

    def combine1(w):
        for d in range(2):
            m1_copy(w, d).wait_recv()
        for d in range(2):
            rows = slice(16 * d, 16 * d + 16)
            total = zown[w, rows] + e1r[w, 1 - d, 16:32].astype(F32)
            total = total + m1r[w, d].astype(F32)
            e2s[w, 2 * d : 2 * d + 2] = total.reshape(2, 8, W)
        for a in (2, 1, 3):
            e2_copy(w, a).start()

    def deliver_copy(w, zz):
        u, g, mb, q = split(w)
        i = q + 4 * g
        dev = (i, (y * 2 + zz) * 4 + x)
        away = (i != dp) | (zh != zz)
        return away, remote(
            fs.at[w, zz], fr.at[mb, dp, zh], s_x.at[w, zz], r_x.at[mb, dp, zh], dev
        )

    def combine2(w):
        u, g, mb, q = split(w)
        top = lax.broadcasted_iota(jnp.int32, (8, WF), 0) < 4
        for a in (1, 3, 2):
            e2_copy(w, a).wait_recv()
        total = e2s[w, jnp.where(g == 0, y, x)]
        for a in range(3):
            total = total + e2r[w, a]
        lo = total[:, 0:WF]
        hi = jnp.concatenate([total[:, WF:W], jnp.zeros((8, 2 * WF - W), F32)], axis=1)
        fs[w, 0] = jnp.where(top, lo, pltpu.roll(hi, 4, 0))
        fs[w, 1] = jnp.where(top, pltpu.roll(lo, 4, 0), hi)
        for zz in range(2):
            away, cp = deliver_copy(w, zz)

            @pl.when(away)
            def _():
                cp.start()

            @pl.when(jnp.logical_not(away))
            def _():
                fr[mb, dp, zh] = fs[w, zz]

    def finish(mb):
        for a in range(NDP):
            for b in range(2):
                if a or b:
                    j, zz = rem(dp + NDP - a, NDP), rem(zh + b, 2)
                    remote(
                        fs.at[0, 0], fr.at[mb, j, zz], s_x.at[0, 0], r_x.at[mb, j, zz], peer
                    ).wait_recv()
        for j in range(NDP):
            total = (fr[mb, j, 0] + fr[mb, j, 1]).astype(BF16)
            out_ref[mb, :, j * W : j * W + WF] = total[0:4]
            out_ref[mb, :, j * W + WF : (j + 1) * W] = total[4:8, 0 : W - WF]

    loads[0].wait()
    dispatch(0)
    for cp in weight_copies():
        cp.start()
    loads[1].wait()
    dispatch(1)
    announce()
    for k in range(4):
        loads[2 + k].wait()
    for k in range(4):
        ref, at = weight_at(k)
        remote(
            ref.at[0, :, hidden_at(oc, k // 2)], wgu.at[oc, :, at], s_w.at[k], r_w.at[k], peer
        ).wait_recv()
    collect(0)
    for n in range(4):
        project_in(0, n)

    @pl.loop(0, 4)
    def _(t):
        chain_step(t)

    collect(1)
    for n in range(4):
        chain_step(4 + n)
        project_in(1, n)
    loads[6].wait()
    for n in range(6):
        remote(rts, rtr.at[source[n]], s_rt.at[n], r_rt.at[source[n]], peer).wait_recv()
    remote(rts, rtr.at[zl * 2 + oc], s_rt.at[6], r_rt.at[zl * 2 + oc], peer).wait_recv()

    @pl.loop(8, PIECES + LAG3)
    def _(t):
        chain_step(t)

        @pl.when(t >= LAG3)
        def _():
            combine2(t - LAG3)

        @pl.when((t >= LAG2) & (t < LAG2 + PIECES))
        def _():
            combine1(t - LAG2)

        @pl.when((t >= LAG1) & (t < LAG1 + PIECES))
        def _():
            merge(t - LAG1)

        @pl.when((t >= LAG0) & (t < LAG0 + PIECES))
        def _():
            spread(t - LAG0)

    finish(0)
    finish(1)

    for cp in weight_copies() + info_copies():
        cp.wait_send()
    chain_sends()
    for mb in range(MB):
        own_copy(mb).wait_send()
        for n in range(6):
            piece_copy(mb, n).wait_send()
            forward_copy(mb, n).wait_send()

    @pl.loop(0, PIECES)
    def _(w):
        for d in range(2):
            e1_copy(w, d).wait_send()
            m1_copy(w, d).wait_send()
        for a in range(1, 4):
            e2_copy(w, a).wait_send()
        for zz in range(2):
            away, cp = deliver_copy(w, zz)

            @pl.when(away)
            def _():
                cp.wait_send()


def per_device(tokens, scores, expert_ids, slot_expert, w_gate, w_up, w_down):
    vmem = pl.BlockSpec(memory_space=pltpu.VMEM)
    anywhere = pl.BlockSpec(memory_space=pl.ANY)
    dma = pltpu.SemaphoreType.DMA
    return pl.pallas_call(
        kernel,
        out_shape=jax.ShapeDtypeStruct((MB, 4, D), BF16),
        in_specs=[
            anywhere, vmem, vmem, pl.BlockSpec(memory_space=pltpu.SMEM),
            anywhere, anywhere, anywhere,
        ],
        out_specs=vmem,
        scratch_shapes=[
            pltpu.VMEM((MB, ROWS, D), BF16),
            pltpu.VMEM((2, W, H), BF16),
            pltpu.VMEM((H, W), BF16),
            pltpu.VMEM((2, MB, CAP, ROWS), BF16),
            pltpu.VMEM((MB, 6, CAP, W), BF16),
            pltpu.VMEM((MB, 2, NDP, CAP, W), BF16),
            pltpu.VMEM((MB, NDP, 2, CAP, 2 * HQ), F32),
            pltpu.VMEM((2, NCH, CAP, 2 * HQ), BF16),
            pltpu.VMEM((2, NCH, CAP, 2 * HQ), BF16),
            pltpu.VMEM((UNITS, 2, 2, 2, CAP, HQ), BF16),
            pltpu.VMEM((4, 32, W), F32),
            pltpu.VMEM((PIECES, 32, W), F32),
            pltpu.VMEM((PIECES, 2, 16, W), F32),
            pltpu.VMEM((PIECES, 2, 32, W), BF16),
            pltpu.VMEM((PIECES, 2, 32, W), BF16),
            pltpu.VMEM((PIECES, 2, 16, W), BF16),
            pltpu.VMEM((PIECES, 2, 16, W), BF16),
            pltpu.VMEM((PIECES, 4, 8, W), F32),
            pltpu.VMEM((PIECES, 3, 8, W), F32),
            pltpu.VMEM((PIECES, 2, 8, WF), F32),
            pltpu.VMEM((MB, NDP, 2, 8, WF), F32),
            pltpu.VMEM((8, ROWS), F32),
            pltpu.VMEM((NDP, 8, ROWS), F32),
            dma((7,)),
            dma((4,)), dma((4,)),
            dma((7,)), dma((NDP,)),
            dma((MB, 6)), dma((MB, NDP)),
            dma((MB, 6)), dma((MB, NDP)),
            dma((MB,)), dma((MB,)),
            dma((2, NCH)), dma((2, NCH)),
            dma((2, NCH)), dma((2, NCH)),
            dma((2, NCH)), dma((2, NCH)),
            dma((PIECES, 2)), dma((PIECES, 2)),
            dma((PIECES, 2)), dma((PIECES, 2)),
            dma((PIECES, 3)), dma((PIECES, 3)),
            dma((PIECES, 2)), dma((MB, NDP, 2)),
        ],
        compiler_params=pltpu.CompilerParams(
            collective_id=0, has_side_effects=True, vmem_limit_bytes=56 * 2**20
        ),
        name="expert_layer",
    )(
        tokens, jnp.swapaxes(scores, 1, 2), jnp.swapaxes(expert_ids, 1, 2), slot_expert,
        w_gate, w_up, w_down,
    )


def solution(mesh):
    in_specs = (
        P(None, "dp", None),
        P(None, "dp", None),
        P(None, "dp", None),
        P(),
        P("expert", "dp", None),
        P("expert", "dp", None),
        P("expert", None, "dp"),
    )
    out_specs = P(None, ("dp", "expert"), None)
    return jax.shard_map(
        per_device, mesh=mesh, in_specs=in_specs, out_specs=out_specs, check_vma=False
    )
```

```python
import jax
import jax.numpy as jnp
from jax import lax
from jax.experimental import pallas as pl
from jax.experimental.pallas import tpu as pltpu
from jax.sharding import PartitionSpec as P

ROUTE_SCALE = 2.5
MESH = pl.DeviceIdType.MESH
F32 = jnp.float32
BF16 = jnp.bfloat16

MB = 2
ROWS = 128
CAP = 48
D = 7168
W = 896
H = 1024
HH = 512
NDP = 8
HQ = 256
NCH = 16
UNITS = 8
WF = 512
MID = 4
AHEAD = 3
SKEW = 2
PIECES = 16
LAG0 = 6 * SKEW + 2
LAG1 = LAG0 + 4
LAG2 = LAG1 + 4


def div(a, b):
    return lax.div(a, jnp.int32(b))


def rem(a, b):
    return lax.rem(a, jnp.int32(b))


def kernel(
    tok_hbm, scores_ref, ids_ref, slot_ref, wg_hbm, wu_hbm, wd_hbm, out_ref,
    tok, wgu, wd, pick, pk, xin, part, bsend, brecv, hid, yv, zf, zown, e1s, e1r, e2f, e2o, e2s, e2r,
    fs, fr, rts, rtr,
    s_loc, s_w, r_w, s_rt, r_rt, s_a, r_a, s_f, r_f, s_o, r_o,
    s_b, r_b, s_c, r_c, s_p, r_p, s_e1, r_e1, s_e2, r_e2, s_x, r_x,
):
    dp = lax.axis_index("dp")
    ex = lax.axis_index("expert")
    zl, c = div(dp, 2), rem(dp, 2)
    y, zh, x = div(ex, 8), rem(div(ex, 4), 2), rem(ex, 4)
    z = zh * 4 + zl
    oc = 1 - c
    peer = (zl * 2 + oc, ex)

    def column(zz, cc):
        return (rem(zz, 4) * 2 + cc, (y * 2 + div(zz, 4)) * 4 + x)

    def xdev(xx):
        return (dp, (y * 2 + zh) * 4 + xx)

    def ydev(yy):
        return (dp, (yy * 2 + zh) * 4 + x)

    def remote(src, dst, ssem, rsem, dev):
        return pltpu.make_async_remote_copy(
            src_ref=src, dst_ref=dst, send_sem=ssem, recv_sem=rsem,
            device_id=dev, device_id_type=MESH,
        )

    def hidden_at(core, half):
        return pl.ds(pl.multiple_of(core * HH + half * HQ, 128), HQ)

    def weight_at(k):
        return (wg_hbm, wu_hbm)[k % 2], pl.ds(k * HQ, HQ)

    loads = [pltpu.make_async_copy(tok_hbm.at[mb], tok.at[mb], s_loc.at[mb]) for mb in range(MB)]
    for k in range(4):
        ref, at = weight_at(k)
        loads.append(
            pltpu.make_async_copy(
                ref.at[0, :, hidden_at(c, k // 2)], wgu.at[c, :, at], s_loc.at[2 + k]
            )
        )
    loads.append(pltpu.make_async_copy(wd_hbm.at[0], wd, s_loc.at[6]))
    for cp in loads:
        cp.start()

    bar = pltpu.get_barrier_semaphore()
    for a in range(NDP):
        for b in range(2):
            if a or b:
                dev = (rem(dp + a, NDP), (y * 2 + rem(zh + b, 2)) * 4 + x)
                pl.semaphore_signal(bar, inc=1, device_id=dev, device_id_type=MESH)
    for a in range(1, 4):
        pl.semaphore_signal(bar, inc=1, device_id=xdev(rem(x + a, 4)), device_id_type=MESH)
        pl.semaphore_signal(bar, inc=1, device_id=ydev(rem(y + a, 4)), device_id_type=MESH)

    row8 = lax.broadcasted_iota(jnp.int32, (8, ROWS), 0)
    rows = jnp.zeros((8, ROWS), F32)
    for mb in range(MB):
        sc = scores_ref[mb]
        ids = ids_ref[mb]
        wts = ROUTE_SCALE * sc / jnp.sum(sc, axis=0, keepdims=True)
        for zz in range(2):
            logical = slot_ref[(y * 2 + zz) * 4 + x]
            hit = ids == logical
            share = jnp.sum(jnp.where(hit, wts, 0.0), axis=0, keepdims=True)
            there = jnp.sum(jnp.where(hit, 1.0, 0.0), axis=0, keepdims=True)
            rows = jnp.where(row8 == zz * 4 + mb, there, rows)
            rows = jnp.where(row8 == zz * 4 + 2 + mb, share, rows)
    lane = lax.broadcasted_iota(jnp.int32, (ROWS, ROWS), 1)
    sub = lax.broadcasted_iota(jnp.int32, (ROWS, ROWS), 0)
    before = jnp.where(sub < lane, 1.0, 0.0).astype(BF16)
    ranks = jnp.dot(rows.astype(BF16), before, preferred_element_type=F32)
    ranks = jnp.where(rows > 0.0, ranks, -1.0)
    info = jnp.where(rem(row8, 4) < 2, ranks, rows)
    place = lax.broadcasted_iota(jnp.int32, (CAP, ROWS), 0).astype(F32)
    for zz in range(2):
        for mb in range(MB):
            r = zz * 4 + mb
            pick[zz, mb] = jnp.where(place == ranks[r : r + 1], 1.0, 0.0).astype(BF16)

    two = jnp.where(c == 1, z + 2, z + 6)
    dest_z = [rem(two, 8)] * 2 + [rem(z + 1, 8)] * 2 + [rem(z + 7, 8)] * 2
    from_z = [rem(zl + 2, 4)] * 2 + [rem(zl + 1, 4)] * 2 + [rem(zl + 3, 4)] * 2
    source = [from_z[n] * 2 + n % 2 for n in range(6)]

    def pack(mb, zz, j):
        piece = tok[mb, :, pl.ds(pl.multiple_of(j * W, 128), W)]
        return jnp.dot(pick[zz, mb], piece, preferred_element_type=F32).astype(BF16)

    def piece_copy(mb, n):
        return remote(
            pk.at[mb, n], xin.at[mb, n % 2, dp], s_a.at[mb, n], r_a.at[mb, dp],
            column(dest_z[n], n % 2),
        )

    def forward_copy(mb, n):
        i = source[n]
        return remote(xin.at[mb, c, i], xin.at[mb, c, i], s_f.at[mb, n], r_f.at[mb, i], peer)

    def own_copy(mb):
        return remote(xin.at[mb, :, dp], xin.at[mb, :, dp], s_o.at[mb], r_o.at[mb], peer)

    def weight_copies():
        out = []
        for k in range(4):
            ref, at = weight_at(k)
            out.append(
                remote(
                    ref.at[0, :, hidden_at(oc, k // 2)], wgu.at[c, :, at],
                    s_w.at[k], r_w.at[k], peer,
                )
            )
        return out

    def info_copies():
        out = [
            remote(rts, rtr.at[dp], s_rt.at[n], r_rt.at[dp], column(dest_z[n], n % 2))
            for n in range(6)
        ]
        return out + [remote(rts, rtr.at[dp], s_rt.at[6], r_rt.at[dp], peer)]

    def dispatch(mb):
        for n in range(6):
            pk[mb, n] = pack(mb, div(dest_z[n], 4), rem(dest_z[n], 4) * 2 + n % 2)
            if mb == 0 and n == 0:
                pl.semaphore_wait(bar, 21)
            piece_copy(mb, n).start()
        for k in range(2):
            xin[mb, k, dp] = pack(mb, zh, zl * 2 + k)
        own_copy(mb).start()

    def announce():
        hi, mid = div(lane, 32), rem(div(lane, 8), 4)
        xx = jnp.where(dp < 4, hi, mid)
        yy = jnp.where(dp < 4, mid, hi)
        home = yy * 32 + rem(div(lane, 4), 2) * 16 + xx * 4 + rem(lane, 4)
        order = jnp.where(sub == home, 1.0, 0.0)
        told = jnp.dot(info, order, preferred_element_type=F32, precision=lax.Precision.HIGHEST)
        rts[...] = told
        rtr[dp] = told
        for cp in info_copies():
            cp.start()

    def collect(mb):
        for n in (2, 3, 4, 5, 0, 1):
            i = source[n]
            remote(
                pk.at[mb, n], xin.at[mb, c, i], s_a.at[mb, n], r_a.at[mb, i], peer
            ).wait_recv()
            forward_copy(mb, n).start()
        own = remote(
            xin.at[mb, :, dp], xin.at[mb, :, zl * 2 + oc], s_o.at[mb], r_o.at[mb], peer
        )
        own.wait_recv()
        for n in (2, 3, 4, 5, 0, 1):
            i = source[n]
            remote(
                xin.at[mb, c, i], xin.at[mb, oc, i], s_f.at[mb, n], r_f.at[mb, i], peer
            ).wait_recv()

    def project_in(mb, half):
        at = pl.ds(half * 2 * HQ, 2 * HQ)
        total = jnp.dot(
            xin[mb, 0].reshape(NDP * CAP, W), wgu[0, :, at], preferred_element_type=F32
        ) + jnp.dot(
            xin[mb, 1].reshape(NDP * CAP, W), wgu[1, :, at], preferred_element_type=F32
        )
        part[mb, :, half] = total.reshape(NDP, CAP, 2 * HQ)

    def chain(d, k):
        half, u = rem(k, 2), div(k, 2)
        q, mb = rem(u, 4), div(u, 4)
        p = zl if d == 0 else 3 - zl
        up = (dp + 2 if d == 0 else dp - 2, ex)
        down = (dp - 2 if d == 0 else dp + 2, ex)
        slot = hid.at[u, c, half, 1 - d]
        own = part.at[mb, q + 4 * (1 - d), half]
        sums = remote(bsend.at[d, k], brecv.at[d, k], s_b.at[d], r_b.at[d, k], up)
        relay = remote(slot, slot, s_c.at[d], r_c.at[d, k], down)
        both = hid.at[u, c, :, 1 - d]
        across = remote(both, both, s_p.at[d], r_p.at[d, u], peer)
        return own, slot, p, sums, relay, across

    def chain_start(k):
        for d in range(2):

            @pl.when((zl if d == 0 else 3 - zl) == 0)
            def _():
                own, slot, p, sums, relay, across = chain(d, k)
                bsend[d, k] = own[...].astype(BF16)
                sums.start()

    def chain_step(t):
        for d in range(2):
            p0 = zl if d == 0 else 3 - zl
            k = t - SKEW * p0

            @pl.when((p0 > 0) & (k >= 0) & (k < NCH))
            def _():
                own, slot, p, sums, relay, across = chain(d, k)
                sums.wait_recv()

                @pl.when(p < 3)
                def _():
                    bsend[d, k] = (own[...] + brecv[d, k].astype(F32)).astype(BF16)
                    sums.start()

                @pl.when(p == 3)
                def _():
                    gate = own[:, 0:HQ] + brecv[d, k, :, 0:HQ].astype(F32)
                    lift = own[:, HQ : 2 * HQ] + brecv[d, k, :, HQ : 2 * HQ].astype(F32)
                    slot[...] = (gate / (1.0 + jnp.exp(-gate)) * lift).astype(BF16)
                    relay.start()

                    @pl.when(rem(k, 2) == 1)
                    def _():
                        across.start()

        for d in range(2):
            p0 = zl if d == 0 else 3 - zl
            k2 = t - SKEW * (6 - p0)

            @pl.when((p0 < 3) & (k2 >= 0) & (k2 < NCH))
            def _():
                own, slot, p, sums, relay, across = chain(d, k2)
                relay.wait_recv()

                @pl.when(p > 0)
                def _():
                    relay.start()

                @pl.when(rem(k2, 2) == 1)
                def _():
                    across.start()

    def chain_sends():
        for d in range(2):
            p = zl if d == 0 else 3 - zl
            sent = hid.at[:, c, :, 1 - d]

            @pl.when(p < 3)
            def _():
                remote(bsend.at[d], brecv.at[d], s_b.at[d], r_b.at[d, 0], peer).wait_send()

            @pl.when(p > 0)
            def _():
                remote(sent, sent, s_c.at[d], r_c.at[d, 0], peer).wait_send()

            remote(sent, sent, s_p.at[d], r_p.at[d, 0], peer).wait_send()

    def split(w):
        u, g = div(w, 2), rem(w, 2)
        return u, g, div(u, 4), rem(u, 4)

    def project_out(u):
        for g in range(2):
            there = hid.at[u, oc, :, g]
            remote(there, there, s_p.at[1 - g], r_p.at[1 - g, u], peer).wait_recv()
        total = jnp.zeros((2 * CAP, W), F32)
        for core in range(2):
            for half in range(2):
                total = total + jnp.dot(
                    hid[u, core, half].reshape(2 * CAP, HQ),
                    wd[core * HH + half * HQ : core * HH + (half + 1) * HQ],
                    preferred_element_type=F32,
                )
        yv[...] = total.astype(BF16).reshape(2, CAP, W)

    to_x = [xdev(rem(x + a, 4)) for a in range(4)]
    to_y = [ydev(rem(y + a, 4)) for a in range(4)]

    def along(on_x, a):
        return (dp, jnp.where(on_x, to_x[a][1], to_y[a][1]))

    def e1_copy(w, a):
        g = rem(w, 2)
        to = rem(jnp.where(g == 0, x, y) + a, 4)
        return remote(e1s.at[w, to], e1r.at[w, a - 1], s_e1, r_e1.at[w], along(g == 0, a))

    def e2_copy(w, a):
        g = rem(w, 2)
        to = rem(jnp.where(g == 0, y, x) + a, 4)
        return remote(e2s.at[w, to], e2r.at[w, a - 1], s_e2, r_e2.at[w], along(g == 1, a))

    def spread(w):
        u, g, mb, q = split(w)

        @pl.when(g == 0)
        def _():
            project_out(u)

        spot = lax.broadcasted_iota(jnp.int32, (ROWS, CAP), 1).astype(F32)
        row = lax.broadcasted_iota(jnp.int32, (8, ROWS), 0)
        told = rtr[g * 4 + q]
        rank = jnp.sum(jnp.where(row == zh * 4 + mb, told, 0.0), axis=0, keepdims=True)
        share = jnp.sum(jnp.where(row == zh * 4 + 2 + mb, told, 0.0), axis=0, keepdims=True)
        turned = jnp.transpose(jnp.where(row == 0, rank, share))
        one = jnp.where(turned[:, 0:1] == spot, 1.0, 0.0).astype(BF16)
        value = turned[:, 1:2] * jnp.dot(one, yv[g], preferred_element_type=F32)
        zf[...] = value.reshape(4, 32, W)
        e1s[w] = zf[...].astype(BF16)
        for a in (2, 1, 3):
            e1_copy(w, a).start()
        zown[w] = zf[jnp.where(g == 0, x, y)]

    def combine1(w):
        remote(e1s.at[w, 0:3], e1r.at[w], s_e1, r_e1.at[w], peer).wait_recv()
        for d in range(2):
            rows = slice(16 * d, 16 * d + 16)
            total = zown[w, rows]
            for a in range(3):
                total = total + e1r[w, a, rows].astype(F32)
            for b in range(2):
                e2f[2 * d + b, 0:8] = total[8 * b : 8 * b + 8, 0:WF]
                e2f[2 * d + b, 8:16, 0 : W - WF] = total[8 * b : 8 * b + 8, WF:W]
        e2s[w] = e2f[...].astype(BF16)
        e2o[w] = e2f[jnp.where(rem(w, 2) == 0, y, x)]
        for a in (2, 1, 3):
            e2_copy(w, a).start()

    def deliver_copy(w, zz):
        u, g, mb, q = split(w)
        i = q + 4 * g
        dev = (i, (y * 2 + zz) * 4 + x)
        away = (i != dp) | (zh != zz)
        return away, remote(
            fs.at[w, zz], fr.at[mb, dp * 2 + zh], s_x, r_x.at[mb], dev
        )

    def combine2(w):
        u, g, mb, q = split(w)
        top = lax.broadcasted_iota(jnp.int32, (8, WF), 0) < 4
        remote(e2s.at[w, 0:3], e2r.at[w], s_e2, r_e2.at[w], peer).wait_recv()
        total = e2o[w]
        for a in range(3):
            total = total + e2r[w, a].astype(F32)
        lo, hi = total[0:8], total[8:16]
        fs[w, 0] = jnp.where(top, lo, pltpu.roll(hi, 4, 0))
        fs[w, 1] = jnp.where(top, pltpu.roll(lo, 4, 0), hi)
        for zz in range(2):
            away, cp = deliver_copy(w, zz)

            @pl.when(away)
            def _():
                cp.start()

            @pl.when(jnp.logical_not(away))
            def _():
                fr[mb, dp * 2 + zh] = fs[w, zz]

    def combine_sends():
        remote(e1s.at[:, 0:3], e1r, s_e1, r_e1.at[0], peer).wait_send()
        remote(e2s.at[:, 0:3], e2r, s_e2, r_e2.at[0], peer).wait_send()
        remote(fs.at[0:15], fs.at[0:15], s_x, r_x.at[0], peer).wait_send()

    def finish(mb):
        there = fr.at[mb, 0:15]
        remote(there, there, s_x, r_x.at[mb], peer).wait_recv()
        for j in range(NDP):
            total = (fr[mb, 2 * j] + fr[mb, 2 * j + 1]).astype(BF16)
            out_ref[mb, :, j * W : j * W + WF] = total[0:4]
            out_ref[mb, :, j * W + WF : (j + 1) * W] = total[4:8, 0 : W - WF]

    loads[0].wait()
    dispatch(0)
    for cp in weight_copies():
        cp.start()
    loads[1].wait()
    dispatch(1)
    announce()
    e2f[...] = jnp.zeros((4, 16, WF), F32)
    for k in range(4):
        loads[2 + k].wait()
    for k in range(4):
        ref, at = weight_at(k)
        remote(
            ref.at[0, :, hidden_at(oc, k // 2)], wgu.at[oc, :, at], s_w.at[k], r_w.at[k], peer
        ).wait_recv()
    collect(0)
    project_in(0, 0)
    chain_start(0)
    project_in(0, 1)

    @pl.loop(1, NCH // 2)
    def _(k):
        chain_start(k)

    for t in range(1, MID + 4):
        chain_step(t)
        if t == MID:
            collect(1)
        if t in (MID, MID + 2):
            project_in(1, (t - MID) // 2)

    @pl.loop(NCH // 2, NCH // 2 + AHEAD)
    def _(k):
        chain_start(k)

    loads[6].wait()
    for n in range(6):
        remote(rts, rtr.at[source[n]], s_rt.at[n], r_rt.at[source[n]], peer).wait_recv()
    remote(rts, rtr.at[zl * 2 + oc], s_rt.at[6], r_rt.at[zl * 2 + oc], peer).wait_recv()

    @pl.loop(MID + 4, PIECES + LAG2)
    def _(t):
        chain_step(t)

        @pl.when(t < NCH // 2 - AHEAD + MID + 4)
        def _():
            chain_start(t + NCH // 2 + AHEAD - MID - 4)

        @pl.when(t >= LAG2)
        def _():
            combine2(t - LAG2)

        @pl.when((t >= LAG1) & (t < LAG1 + PIECES))
        def _():
            combine1(t - LAG1)

        @pl.when((t >= LAG0) & (t < LAG0 + PIECES))
        def _():
            spread(t - LAG0)

    finish(0)
    finish(1)

    chain_sends()
    combine_sends()
    for cp in weight_copies() + info_copies():
        cp.wait_send()
    for mb in range(MB):
        own_copy(mb).wait_send()
        for n in range(6):
            piece_copy(mb, n).wait_send()
            forward_copy(mb, n).wait_send()


def per_device(tokens, scores, expert_ids, slot_expert, w_gate, w_up, w_down):
    vmem = pl.BlockSpec(memory_space=pltpu.VMEM)
    anywhere = pl.BlockSpec(memory_space=pl.ANY)
    dma = pltpu.SemaphoreType.DMA
    return pl.pallas_call(
        kernel,
        out_shape=jax.ShapeDtypeStruct((MB, 4, D), BF16),
        in_specs=[
            anywhere, vmem, vmem, pl.BlockSpec(memory_space=pltpu.SMEM),
            anywhere, anywhere, anywhere,
        ],
        out_specs=vmem,
        scratch_shapes=[
            pltpu.VMEM((MB, ROWS, D), BF16),
            pltpu.VMEM((2, W, H), BF16),
            pltpu.VMEM((H, W), BF16),
            pltpu.VMEM((2, MB, CAP, ROWS), BF16),
            pltpu.VMEM((MB, 6, CAP, W), BF16),
            pltpu.VMEM((MB, 2, NDP, CAP, W), BF16),
            pltpu.VMEM((MB, NDP, 2, CAP, 2 * HQ), F32),
            pltpu.VMEM((2, NCH, CAP, 2 * HQ), BF16),
            pltpu.VMEM((2, NCH, CAP, 2 * HQ), BF16),
            pltpu.VMEM((UNITS, 2, 2, 2, CAP, HQ), BF16),
            pltpu.VMEM((2, CAP, W), BF16),
            pltpu.VMEM((4, 32, W), F32),
            pltpu.VMEM((PIECES, 32, W), F32),
            pltpu.VMEM((PIECES, 4, 32, W), BF16),
            pltpu.VMEM((PIECES, 3, 32, W), BF16),
            pltpu.VMEM((4, 16, WF), F32),
            pltpu.VMEM((PIECES, 16, WF), F32),
            pltpu.VMEM((PIECES, 4, 16, WF), BF16),
            pltpu.VMEM((PIECES, 3, 16, WF), BF16),
            pltpu.VMEM((PIECES, 2, 8, WF), F32),
            pltpu.VMEM((MB, 2 * NDP, 8, WF), F32),
            pltpu.VMEM((8, ROWS), F32),
            pltpu.VMEM((NDP, 8, ROWS), F32),
            dma((7,)),
            dma((4,)), dma((4,)),
            dma((7,)), dma((NDP,)),
            dma((MB, 6)), dma((MB, NDP)),
            dma((MB, 6)), dma((MB, NDP)),
            dma((MB,)), dma((MB,)),
            dma((2,)), dma((2, NCH)),
            dma((2,)), dma((2, NCH)),
            dma((2,)), dma((2, UNITS)),
            dma, dma((PIECES,)),
            dma, dma((PIECES,)),
            dma, dma((MB,)),
        ],
        compiler_params=pltpu.CompilerParams(
            collective_id=0, has_side_effects=True, vmem_limit_bytes=56 * 2**20
        ),
        name="expert_layer",
    )(
        tokens, jnp.swapaxes(scores, 1, 2), jnp.swapaxes(expert_ids, 1, 2), slot_expert,
        w_gate, w_up, w_down,
    )


def solution(mesh):
    in_specs = (
        P(None, "dp", None),
        P(None, "dp", None),
        P(None, "dp", None),
        P(),
        P("expert", "dp", None),
        P("expert", "dp", None),
        P("expert", None, "dp"),
    )
    out_specs = P(None, ("dp", "expert"), None)
    return jax.shard_map(
        per_device, mesh=mesh, in_specs=in_specs, out_specs=out_specs, check_vma=False
    )
```

```python
import jax
import jax.numpy as jnp
from jax import lax
from jax.experimental import pallas as pl
from jax.experimental.pallas import tpu as pltpu
from jax.sharding import PartitionSpec as P

ROUTE_SCALE = 2.5
MESH = pl.DeviceIdType.MESH
F32 = jnp.float32
BF16 = jnp.bfloat16

MB = 2
ROWS = 128
CAP = 48
D = 7168
W = 896
H = 1024
HH = 512
NDP = 8
HQ = 256
NCH = 16
UNITS = 8
WF = 512
MID = 4
AHEAD = 3
SKEW = 3
BACK = 2
PIECES = 16
LAG0 = 3 * (SKEW + BACK) + 1
LAG1 = LAG0 + 4
LAG2 = LAG1 + 4


def div(a, b):
    return lax.div(a, jnp.int32(b))


def rem(a, b):
    return lax.rem(a, jnp.int32(b))


def kernel(
    tok_hbm, scores_ref, ids_ref, slot_ref, wg_hbm, wu_hbm, wd_hbm, out_ref,
    tok, wgu, wd, pick, pk, xin, part, bsend, brecv, hid, yv, zf, zown, e1s, e1r, e2f, e2o, e2s, e2r,
    fs, fr, rts, rtr,
    s_loc, s_w, r_w, s_rt, r_rt, s_a, r_a, s_f, r_f, s_o, r_o,
    s_b, r_b, s_c, r_c, s_p, r_p, s_e1, r_e1, s_e2, r_e2, s_x, r_x,
):
    dp = lax.axis_index("dp")
    ex = lax.axis_index("expert")
    zl, c = div(dp, 2), rem(dp, 2)
    y, zh, x = div(ex, 8), rem(div(ex, 4), 2), rem(ex, 4)
    z = zh * 4 + zl
    oc = 1 - c
    peer = (zl * 2 + oc, ex)

    def column(zz, cc):
        return (rem(zz, 4) * 2 + cc, (y * 2 + div(zz, 4)) * 4 + x)

    def xdev(xx):
        return (dp, (y * 2 + zh) * 4 + xx)

    def ydev(yy):
        return (dp, (yy * 2 + zh) * 4 + x)

    def remote(src, dst, ssem, rsem, dev):
        return pltpu.make_async_remote_copy(
            src_ref=src, dst_ref=dst, send_sem=ssem, recv_sem=rsem,
            device_id=dev, device_id_type=MESH,
        )

    def hidden_at(core, half):
        return pl.ds(pl.multiple_of(core * HH + half * HQ, 128), HQ)

    def weight_at(k):
        return (wg_hbm, wu_hbm)[k % 2], pl.ds(k * HQ, HQ)

    loads = [pltpu.make_async_copy(tok_hbm.at[mb], tok.at[mb], s_loc.at[mb]) for mb in range(MB)]
    for k in range(4):
        ref, at = weight_at(k)
        loads.append(
            pltpu.make_async_copy(
                ref.at[0, :, hidden_at(c, k // 2)], wgu.at[c, :, at], s_loc.at[2 + k]
            )
        )
    loads.append(pltpu.make_async_copy(wd_hbm.at[0], wd, s_loc.at[6]))
    for cp in loads:
        cp.start()

    bar = pltpu.get_barrier_semaphore()
    for a in range(NDP):
        for b in range(2):
            if a or b:
                dev = (rem(dp + a, NDP), (y * 2 + rem(zh + b, 2)) * 4 + x)
                pl.semaphore_signal(bar, inc=1, device_id=dev, device_id_type=MESH)
    for a in range(1, 4):
        pl.semaphore_signal(bar, inc=1, device_id=xdev(rem(x + a, 4)), device_id_type=MESH)
        pl.semaphore_signal(bar, inc=1, device_id=ydev(rem(y + a, 4)), device_id_type=MESH)

    row8 = lax.broadcasted_iota(jnp.int32, (8, ROWS), 0)
    rows = jnp.zeros((8, ROWS), F32)
    for mb in range(MB):
        sc = scores_ref[mb]
        ids = ids_ref[mb]
        wts = ROUTE_SCALE * sc / jnp.sum(sc, axis=0, keepdims=True)
        for zz in range(2):
            logical = slot_ref[(y * 2 + zz) * 4 + x]
            hit = ids == logical
            share = jnp.sum(jnp.where(hit, wts, 0.0), axis=0, keepdims=True)
            there = jnp.sum(jnp.where(hit, 1.0, 0.0), axis=0, keepdims=True)
            rows = jnp.where(row8 == zz * 4 + mb, there, rows)
            rows = jnp.where(row8 == zz * 4 + 2 + mb, share, rows)
    lane = lax.broadcasted_iota(jnp.int32, (ROWS, ROWS), 1)
    sub = lax.broadcasted_iota(jnp.int32, (ROWS, ROWS), 0)
    before = jnp.where(sub < lane, 1.0, 0.0).astype(BF16)
    ranks = jnp.dot(rows.astype(BF16), before, preferred_element_type=F32)
    ranks = jnp.where(rows > 0.0, ranks, -1.0)
    info = jnp.where(rem(row8, 4) < 2, ranks, rows)
    place = lax.broadcasted_iota(jnp.int32, (CAP, ROWS), 0).astype(F32)
    for zz in range(2):
        for mb in range(MB):
            r = zz * 4 + mb
            pick[zz, mb] = jnp.where(place == ranks[r : r + 1], 1.0, 0.0).astype(BF16)

    two = jnp.where(c == 1, z + 2, z + 6)
    dest_z = [rem(two, 8)] * 2 + [rem(z + 1, 8)] * 2 + [rem(z + 7, 8)] * 2
    from_z = [rem(zl + 2, 4)] * 2 + [rem(zl + 1, 4)] * 2 + [rem(zl + 3, 4)] * 2
    source = [from_z[n] * 2 + n % 2 for n in range(6)]

    def pack(mb, zz, j):
        piece = tok[mb, :, pl.ds(pl.multiple_of(j * W, 128), W)]
        return jnp.dot(pick[zz, mb], piece, preferred_element_type=F32).astype(BF16)

    def piece_copy(mb, n):
        return remote(
            pk.at[mb, n], xin.at[mb, n % 2, dp], s_a.at[mb, n], r_a.at[mb, dp],
            column(dest_z[n], n % 2),
        )

    def forward_copy(mb, n):
        i = source[n]
        return remote(xin.at[mb, c, i], xin.at[mb, c, i], s_f.at[mb, n], r_f.at[mb, i], peer)

    def own_copy(mb):
        return remote(xin.at[mb, :, dp], xin.at[mb, :, dp], s_o.at[mb], r_o.at[mb], peer)

    def weight_copies():
        out = []
        for k in range(4):
            ref, at = weight_at(k)
            out.append(
                remote(
                    ref.at[0, :, hidden_at(oc, k // 2)], wgu.at[c, :, at],
                    s_w.at[k], r_w.at[k], peer,
                )
            )
        return out

    def info_copies():
        out = [
            remote(rts, rtr.at[dp], s_rt.at[n], r_rt.at[dp], column(dest_z[n], n % 2))
            for n in range(6)
        ]
        return out + [remote(rts, rtr.at[dp], s_rt.at[6], r_rt.at[dp], peer)]

    def dispatch(mb):
        for n in range(6):
            pk[mb, n] = pack(mb, div(dest_z[n], 4), rem(dest_z[n], 4) * 2 + n % 2)
            if mb == 0 and n == 0:
                pl.semaphore_wait(bar, 21)
            piece_copy(mb, n).start()
        for k in range(2):
            xin[mb, k, dp] = pack(mb, zh, zl * 2 + k)
        own_copy(mb).start()

    def announce():
        hi, mid = div(lane, 32), rem(div(lane, 8), 4)
        xx = jnp.where(dp < 4, hi, mid)
        yy = jnp.where(dp < 4, mid, hi)
        home = yy * 32 + rem(div(lane, 4), 2) * 16 + xx * 4 + rem(lane, 4)
        order = jnp.where(sub == home, 1.0, 0.0)
        told = jnp.dot(info, order, preferred_element_type=F32, precision=lax.Precision.HIGHEST)
        rts[...] = told
        rtr[dp] = told
        for cp in info_copies():
            cp.start()

    def collect(mb):
        for n in (2, 3, 4, 5, 0, 1):
            i = source[n]
            remote(
                pk.at[mb, n], xin.at[mb, c, i], s_a.at[mb, n], r_a.at[mb, i], peer
            ).wait_recv()
            forward_copy(mb, n).start()
        own = remote(
            xin.at[mb, :, dp], xin.at[mb, :, zl * 2 + oc], s_o.at[mb], r_o.at[mb], peer
        )
        own.wait_recv()
        for n in (2, 3, 4, 5, 0, 1):
            i = source[n]
            remote(
                xin.at[mb, c, i], xin.at[mb, oc, i], s_f.at[mb, n], r_f.at[mb, i], peer
            ).wait_recv()

    def project_in(mb, half):
        at = pl.ds(half * 2 * HQ, 2 * HQ)
        rows_in = jnp.concatenate([xin[mb, k].reshape(NDP * CAP, W) for k in range(2)], axis=1)
        total = jnp.dot(
            rows_in, wgu[:, :, at].reshape(2 * W, 2 * HQ), preferred_element_type=F32
        )
        part[mb, :, half] = total.reshape(NDP, CAP, 2 * HQ)

    def chain(d, k):
        half, u = rem(k, 2), div(k, 2)
        q, mb = rem(u, 4), div(u, 4)
        p = zl if d == 0 else 3 - zl
        up = (dp + 2 if d == 0 else dp - 2, ex)
        down = (dp - 2 if d == 0 else dp + 2, ex)
        slot = hid.at[u, c, half, 1 - d]
        own = part.at[mb, q + 4 * (1 - d), half]
        sums = remote(bsend.at[d, k], brecv.at[d, k], s_b.at[d], r_b.at[d, k], up)
        relay = remote(slot, slot, s_c.at[d], r_c.at[d, k], down)
        both = hid.at[u, c, :, 1 - d]
        across = remote(both, both, s_p.at[d], r_p.at[d, u], peer)
        return own, slot, p, sums, relay, across

    def chain_start(k):
        for d in range(2):

            @pl.when((zl if d == 0 else 3 - zl) == 0)
            def _():
                own, slot, p, sums, relay, across = chain(d, k)
                bsend[d, k] = own[...].astype(BF16)
                sums.start()

    def chain_step(t):
        for d in range(2):
            p0 = zl if d == 0 else 3 - zl
            k = t - SKEW * p0

            @pl.when((p0 > 0) & (k >= 0) & (k < NCH))
            def _():
                own, slot, p, sums, relay, across = chain(d, k)
                sums.wait_recv()

                @pl.when(p < 3)
                def _():
                    bsend[d, k] = (own[...] + brecv[d, k].astype(F32)).astype(BF16)
                    sums.start()

                @pl.when(p == 3)
                def _():
                    gate = own[:, 0:HQ] + brecv[d, k, :, 0:HQ].astype(F32)
                    lift = own[:, HQ : 2 * HQ] + brecv[d, k, :, HQ : 2 * HQ].astype(F32)
                    slot[...] = (gate / (1.0 + jnp.exp(-gate)) * lift).astype(BF16)
                    relay.start()

                    @pl.when(rem(k, 2) == 1)
                    def _():
                        across.start()

        for d in range(2):
            p0 = zl if d == 0 else 3 - zl
            k2 = t - 3 * SKEW - BACK * (3 - p0)

            @pl.when((p0 < 3) & (k2 >= 0) & (k2 < NCH))
            def _():
                own, slot, p, sums, relay, across = chain(d, k2)
                relay.wait_recv()

                @pl.when(p > 0)
                def _():
                    relay.start()

                @pl.when(rem(k2, 2) == 1)
                def _():
                    across.start()

    def chain_sends():
        for d in range(2):
            p = zl if d == 0 else 3 - zl
            sent = hid.at[:, c, :, 1 - d]

            @pl.when(p < 3)
            def _():
                remote(bsend.at[d], brecv.at[d], s_b.at[d], r_b.at[d, 0], peer).wait_send()

            @pl.when(p > 0)
            def _():
                remote(sent, sent, s_c.at[d], r_c.at[d, 0], peer).wait_send()

            remote(sent, sent, s_p.at[d], r_p.at[d, 0], peer).wait_send()

    def split(w):
        u, g = div(w, 2), rem(w, 2)
        return u, g, div(u, 4), rem(u, 4)

    def project_out(u):
        for g in range(2):
            there = hid.at[u, oc, :, g]
            remote(there, there, s_p.at[1 - g], r_p.at[1 - g, u], peer).wait_recv()
        parts = [hid[u, core, half].reshape(2 * CAP, HQ) for core in range(2) for half in range(2)]
        total = jnp.dot(
            jnp.concatenate(parts, axis=1), wd[...], preferred_element_type=F32
        )
        yv[...] = total.astype(BF16).reshape(2, CAP, W)

    to_x = [xdev(rem(x + a, 4)) for a in range(4)]
    to_y = [ydev(rem(y + a, 4)) for a in range(4)]

    def along(on_x, a):
        return (dp, jnp.where(on_x, to_x[a][1], to_y[a][1]))

    def e1_copy(w, a):
        g = rem(w, 2)
        to = rem(jnp.where(g == 0, x, y) + a, 4)
        return remote(e1s.at[w, to], e1r.at[w, a - 1], s_e1, r_e1.at[w], along(g == 0, a))

    def e2_copy(w, a):
        g = rem(w, 2)
        to = rem(jnp.where(g == 0, y, x) + a, 4)
        return remote(e2s.at[w, to], e2r.at[w, a - 1], s_e2, r_e2.at[w], along(g == 1, a))

    def spread(w):
        u, g, mb, q = split(w)

        @pl.when(g == 0)
        def _():
            project_out(u)

        spot = lax.broadcasted_iota(jnp.int32, (ROWS, CAP), 1).astype(F32)
        row = lax.broadcasted_iota(jnp.int32, (8, ROWS), 0)
        told = rtr[g * 4 + q]
        rank = jnp.sum(jnp.where(row == zh * 4 + mb, told, 0.0), axis=0, keepdims=True)
        share = jnp.sum(jnp.where(row == zh * 4 + 2 + mb, told, 0.0), axis=0, keepdims=True)
        turned = jnp.transpose(jnp.where(row == 0, rank, share))
        one = jnp.where(turned[:, 0:1] == spot, 1.0, 0.0).astype(BF16)
        value = turned[:, 1:2] * jnp.dot(one, yv[g], preferred_element_type=F32)
        value = value.reshape(4, 32, W)
        e1s[w] = value.astype(BF16)
        zf[...] = value
        for a in (2, 1, 3):
            e1_copy(w, a).start()
        zown[w] = zf[jnp.where(g == 0, x, y)]

    def combine1(w):
        remote(e1s.at[w, 0:3], e1r.at[w], s_e1, r_e1.at[w], peer).wait_recv()
        for d in range(2):
            rows = slice(16 * d, 16 * d + 16)
            total = zown[w, rows]
            for a in range(3):
                total = total + e1r[w, a, rows].astype(F32)
            for b in range(2):
                e2f[2 * d + b, 0:8] = total[8 * b : 8 * b + 8, 0:WF]
                e2f[2 * d + b, 8:16, 0 : W - WF] = total[8 * b : 8 * b + 8, WF:W]
        e2s[w] = e2f[...].astype(BF16)
        e2o[w] = e2f[jnp.where(rem(w, 2) == 0, y, x)]
        for a in (2, 1, 3):
            e2_copy(w, a).start()

    def deliver_copy(w, zz):
        u, g, mb, q = split(w)
        i = q + 4 * g
        dev = (i, (y * 2 + zz) * 4 + x)
        away = (i != dp) | (zh != zz)
        return away, remote(
            fs.at[w, zz], fr.at[mb, dp * 2 + zh], s_x, r_x.at[mb], dev
        )

    def combine2(w):
        u, g, mb, q = split(w)
        top = lax.broadcasted_iota(jnp.int32, (8, WF), 0) < 4
        remote(e2s.at[w, 0:3], e2r.at[w], s_e2, r_e2.at[w], peer).wait_recv()
        total = e2o[w]
        for a in range(3):
            total = total + e2r[w, a].astype(F32)
        lo, hi = total[0:8], total[8:16]
        fs[w, 0] = jnp.where(top, lo, pltpu.roll(hi, 4, 0))
        fs[w, 1] = jnp.where(top, pltpu.roll(lo, 4, 0), hi)
        for zz in range(2):
            away, cp = deliver_copy(w, zz)

            @pl.when(away)
            def _():
                cp.start()

            @pl.when(jnp.logical_not(away))
            def _():
                fr[mb, dp * 2 + zh] = fs[w, zz]

    def combine_sends():
        remote(e1s.at[:, 0:3], e1r, s_e1, r_e1.at[0], peer).wait_send()
        remote(e2s.at[:, 0:3], e2r, s_e2, r_e2.at[0], peer).wait_send()
        remote(fs.at[0:15], fs.at[0:15], s_x, r_x.at[0], peer).wait_send()

    def finish(mb):
        there = fr.at[mb, 0:15]
        remote(there, there, s_x, r_x.at[mb], peer).wait_recv()
        for j in range(NDP):
            total = (fr[mb, 2 * j] + fr[mb, 2 * j + 1]).astype(BF16)
            out_ref[mb, :, j * W : j * W + WF] = total[0:4]
            out_ref[mb, :, j * W + WF : (j + 1) * W] = total[4:8, 0 : W - WF]

    loads[0].wait()
    dispatch(0)
    for cp in weight_copies():
        cp.start()
    loads[1].wait()
    dispatch(1)
    announce()
    e2f[...] = jnp.zeros((4, 16, WF), F32)
    for k in range(4):
        loads[2 + k].wait()
    for k in range(4):
        ref, at = weight_at(k)
        remote(
            ref.at[0, :, hidden_at(oc, k // 2)], wgu.at[oc, :, at], s_w.at[k], r_w.at[k], peer
        ).wait_recv()
    collect(0)
    project_in(0, 0)
    chain_start(0)
    project_in(0, 1)

    @pl.loop(1, NCH // 2)
    def _(k):
        chain_start(k)

    for t in range(1, MID + 4):
        chain_step(t)
        if t == MID:
            collect(1)
        if t in (MID, MID + 2):
            project_in(1, (t - MID) // 2)

    @pl.loop(NCH // 2, NCH // 2 + AHEAD)
    def _(k):
        chain_start(k)

    loads[6].wait()
    for n in range(6):
        remote(rts, rtr.at[source[n]], s_rt.at[n], r_rt.at[source[n]], peer).wait_recv()
    remote(rts, rtr.at[zl * 2 + oc], s_rt.at[6], r_rt.at[zl * 2 + oc], peer).wait_recv()

    @pl.loop(MID + 4, PIECES + LAG2)
    def _(t):
        chain_step(t)

        @pl.when(t < NCH // 2 - AHEAD + MID + 4)
        def _():
            chain_start(t + NCH // 2 + AHEAD - MID - 4)

        @pl.when(t >= LAG2)
        def _():
            combine2(t - LAG2)

        @pl.when((t >= LAG1) & (t < LAG1 + PIECES))
        def _():
            combine1(t - LAG1)

        @pl.when((t >= LAG0) & (t < LAG0 + PIECES))
        def _():
            spread(t - LAG0)

    finish(0)
    finish(1)

    chain_sends()
    combine_sends()
    for cp in weight_copies() + info_copies():
        cp.wait_send()
    for mb in range(MB):
        own_copy(mb).wait_send()
        for n in range(6):
            piece_copy(mb, n).wait_send()
            forward_copy(mb, n).wait_send()


def per_device(tokens, scores, expert_ids, slot_expert, w_gate, w_up, w_down):
    vmem = pl.BlockSpec(memory_space=pltpu.VMEM)
    anywhere = pl.BlockSpec(memory_space=pl.ANY)
    dma = pltpu.SemaphoreType.DMA
    return pl.pallas_call(
        kernel,
        out_shape=jax.ShapeDtypeStruct((MB, 4, D), BF16),
        in_specs=[
            anywhere, vmem, vmem, pl.BlockSpec(memory_space=pltpu.SMEM),
            anywhere, anywhere, anywhere,
        ],
        out_specs=vmem,
        scratch_shapes=[
            pltpu.VMEM((MB, ROWS, D), BF16),
            pltpu.VMEM((2, W, H), BF16),
            pltpu.VMEM((H, W), BF16),
            pltpu.VMEM((2, MB, CAP, ROWS), BF16),
            pltpu.VMEM((MB, 6, CAP, W), BF16),
            pltpu.VMEM((MB, 2, NDP, CAP, W), BF16),
            pltpu.VMEM((MB, NDP, 2, CAP, 2 * HQ), F32),
            pltpu.VMEM((2, NCH, CAP, 2 * HQ), BF16),
            pltpu.VMEM((2, NCH, CAP, 2 * HQ), BF16),
            pltpu.VMEM((UNITS, 2, 2, 2, CAP, HQ), BF16),
            pltpu.VMEM((2, CAP, W), BF16),
            pltpu.VMEM((4, 32, W), F32),
            pltpu.VMEM((PIECES, 32, W), F32),
            pltpu.VMEM((PIECES, 4, 32, W), BF16),
            pltpu.VMEM((PIECES, 3, 32, W), BF16),
            pltpu.VMEM((4, 16, WF), F32),
            pltpu.VMEM((PIECES, 16, WF), F32),
            pltpu.VMEM((PIECES, 4, 16, WF), BF16),
            pltpu.VMEM((PIECES, 3, 16, WF), BF16),
            pltpu.VMEM((PIECES, 2, 8, WF), F32),
            pltpu.VMEM((MB, 2 * NDP, 8, WF), F32),
            pltpu.VMEM((8, ROWS), F32),
            pltpu.VMEM((NDP, 8, ROWS), F32),
            dma((7,)),
            dma((4,)), dma((4,)),
            dma((7,)), dma((NDP,)),
            dma((MB, 6)), dma((MB, NDP)),
            dma((MB, 6)), dma((MB, NDP)),
            dma((MB,)), dma((MB,)),
            dma((2,)), dma((2, NCH)),
            dma((2,)), dma((2, NCH)),
            dma((2,)), dma((2, UNITS)),
            dma, dma((PIECES,)),
            dma, dma((PIECES,)),
            dma, dma((MB,)),
        ],
        compiler_params=pltpu.CompilerParams(
            collective_id=0, has_side_effects=True, vmem_limit_bytes=56 * 2**20
        ),
        name="expert_layer",
    )(
        tokens, jnp.swapaxes(scores, 1, 2), jnp.swapaxes(expert_ids, 1, 2), slot_expert,
        w_gate, w_up, w_down,
    )


def solution(mesh):
    in_specs = (
        P(None, "dp", None),
        P(None, "dp", None),
        P(None, "dp", None),
        P(),
        P("expert", "dp", None),
        P("expert", "dp", None),
        P("expert", None, "dp"),
    )
    out_specs = P(None, ("dp", "expert"), None)
    return jax.shard_map(
        per_device, mesh=mesh, in_specs=in_specs, out_specs=out_specs, check_vma=False
    )
```

```python
import jax
import jax.numpy as jnp
from jax import lax
from jax.experimental import pallas as pl
from jax.experimental.pallas import tpu as pltpu
from jax.sharding import PartitionSpec as P

ROUTE_SCALE = 2.5
MESH = pl.DeviceIdType.MESH
F32 = jnp.float32
BF16 = jnp.bfloat16

MB = 2
ROWS = 128
CAP = 48
D = 7168
W = 896
H = 1024
HH = 512
NDP = 8
HQ = 256
NCH = 16
UNITS = 8
WF = 512
MID = 4
AHEAD = 3
SKEW = 3
BACK = 2
PIECES = 16
LAG0 = 3 * (SKEW + BACK) + 1
LAG1 = LAG0 + 4
LAG2 = LAG1 + 4


def div(a, b):
    return lax.div(a, jnp.int32(b))


def rem(a, b):
    return lax.rem(a, jnp.int32(b))


def kernel(
    tok_hbm, scores_ref, ids_ref, slot_ref, wg_hbm, wu_hbm, wd_hbm, out_ref,
    tok, wgu, wd, pick, pk, xin, part, bsend, brecv, hid, yv, zf, zown, e1s, e1r, e2f, e2o, e2s, e2r,
    fs, fr, rts, rtr,
    s_loc, s_w, r_w, s_rt, r_rt, s_a, r_a, s_f, r_f, s_o, r_o,
    s_b, r_b, s_c, r_c, s_p, r_p, s_e1, r_e1, s_e2, r_e2, s_x, r_x,
):
    dp = lax.axis_index("dp")
    ex = lax.axis_index("expert")
    zl, c = div(dp, 2), rem(dp, 2)
    y, zh, x = div(ex, 8), rem(div(ex, 4), 2), rem(ex, 4)
    z = zh * 4 + zl
    oc = 1 - c
    peer = (zl * 2 + oc, ex)

    def column(zz, cc):
        return (rem(zz, 4) * 2 + cc, (y * 2 + div(zz, 4)) * 4 + x)

    def xdev(xx):
        return (dp, (y * 2 + zh) * 4 + xx)

    def ydev(yy):
        return (dp, (yy * 2 + zh) * 4 + x)

    def remote(src, dst, ssem, rsem, dev):
        return pltpu.make_async_remote_copy(
            src_ref=src, dst_ref=dst, send_sem=ssem, recv_sem=rsem,
            device_id=dev, device_id_type=MESH,
        )

    def hidden_at(core, half):
        return pl.ds(pl.multiple_of(core * HH + half * HQ, 128), HQ)

    def weight_at(k):
        return (wg_hbm, wu_hbm)[k % 2], pl.ds(k * HQ, HQ)

    loads = [pltpu.make_async_copy(tok_hbm.at[mb], tok.at[mb], s_loc.at[mb]) for mb in range(MB)]
    for k in range(4):
        ref, at = weight_at(k)
        loads.append(
            pltpu.make_async_copy(
                ref.at[0, :, hidden_at(c, k // 2)], wgu.at[c, :, at], s_loc.at[2 + k]
            )
        )
    loads.append(pltpu.make_async_copy(wd_hbm.at[0], wd, s_loc.at[6]))
    for cp in loads:
        cp.start()

    bar = pltpu.get_barrier_semaphore()
    for a in range(NDP):
        for b in range(2):
            if a or b:
                dev = (rem(dp + a, NDP), (y * 2 + rem(zh + b, 2)) * 4 + x)
                pl.semaphore_signal(bar, inc=1, device_id=dev, device_id_type=MESH)
    for a in range(1, 4):
        pl.semaphore_signal(bar, inc=1, device_id=xdev(rem(x + a, 4)), device_id_type=MESH)
        pl.semaphore_signal(bar, inc=1, device_id=ydev(rem(y + a, 4)), device_id_type=MESH)

    row8 = lax.broadcasted_iota(jnp.int32, (8, ROWS), 0)
    rows = jnp.zeros((8, ROWS), F32)
    for mb in range(MB):
        sc = scores_ref[mb]
        ids = ids_ref[mb]
        wts = ROUTE_SCALE * sc / jnp.sum(sc, axis=0, keepdims=True)
        for zz in range(2):
            logical = slot_ref[(y * 2 + zz) * 4 + x]
            hit = ids == logical
            share = jnp.sum(jnp.where(hit, wts, 0.0), axis=0, keepdims=True)
            there = jnp.sum(jnp.where(hit, 1.0, 0.0), axis=0, keepdims=True)
            rows = jnp.where(row8 == zz * 4 + mb, there, rows)
            rows = jnp.where(row8 == zz * 4 + 2 + mb, share, rows)
    lane = lax.broadcasted_iota(jnp.int32, (ROWS, ROWS), 1)
    sub = lax.broadcasted_iota(jnp.int32, (ROWS, ROWS), 0)
    before = jnp.where(sub < lane, 1.0, 0.0).astype(BF16)
    ranks = jnp.dot(rows.astype(BF16), before, preferred_element_type=F32)
    ranks = jnp.where(rows > 0.0, ranks, -1.0)
    info = jnp.where(rem(row8, 4) < 2, ranks, rows)
    place = lax.broadcasted_iota(jnp.int32, (CAP, ROWS), 0).astype(F32)
    for zz in range(2):
        for mb in range(MB):
            r = zz * 4 + mb
            pick[zz, mb] = jnp.where(place == ranks[r : r + 1], 1.0, 0.0).astype(BF16)

    two = jnp.where(c == 1, z + 2, z + 6)
    dest_z = [rem(two, 8)] * 2 + [rem(z + 1, 8)] * 2 + [rem(z + 7, 8)] * 2
    from_z = [rem(zl + 2, 4)] * 2 + [rem(zl + 1, 4)] * 2 + [rem(zl + 3, 4)] * 2
    source = [from_z[n] * 2 + n % 2 for n in range(6)]

    def pack(mb, zz, j):
        piece = tok[mb, :, pl.ds(pl.multiple_of(j * W, 128), W)]
        return jnp.dot(pick[zz, mb], piece, preferred_element_type=F32).astype(BF16)

    def piece_copy(mb, n):
        return remote(
            pk.at[mb, n], xin.at[mb, n % 2, dp], s_a.at[mb], r_a.at[mb, dp],
            column(dest_z[n], n % 2),
        )

    def forward_copy(mb, n):
        i = source[n]
        return remote(xin.at[mb, c, i], xin.at[mb, c, i], s_f.at[mb], r_f.at[mb], peer)

    def own_copy(mb):
        return remote(xin.at[mb, :, dp], xin.at[mb, :, dp], s_o.at[mb], r_o.at[mb], peer)

    def weight_copies():
        out = []
        for k in range(4):
            ref, at = weight_at(k)
            out.append(
                remote(
                    ref.at[0, :, hidden_at(oc, k // 2)], wgu.at[c, :, at],
                    s_w.at[k], r_w.at[k], peer,
                )
            )
        return out

    def info_copies():
        out = [
            remote(rts, rtr.at[dp], s_rt, r_rt, column(dest_z[n], n % 2))
            for n in range(6)
        ]
        return out + [remote(rts, rtr.at[dp], s_rt, r_rt, peer)]

    def dispatch(mb):
        for n in range(6):
            pk[mb, n] = pack(mb, div(dest_z[n], 4), rem(dest_z[n], 4) * 2 + n % 2)
            if mb == 0 and n == 0:
                pl.semaphore_wait(bar, 21)
            piece_copy(mb, n).start()
        for k in range(2):
            xin[mb, k, dp] = pack(mb, zh, zl * 2 + k)
        own_copy(mb).start()

    def announce():
        hi, mid = div(lane, 32), rem(div(lane, 8), 4)
        xx = jnp.where(dp < 4, hi, mid)
        yy = jnp.where(dp < 4, mid, hi)
        home = yy * 32 + rem(div(lane, 4), 2) * 16 + xx * 4 + rem(lane, 4)
        order = jnp.where(sub == home, 1.0, 0.0)
        told = jnp.dot(info, order, preferred_element_type=F32, precision=lax.Precision.HIGHEST)
        rts[...] = told
        rtr[dp] = told
        for cp in info_copies():
            cp.start()

    def collect(mb):
        for n in (2, 3, 4, 5, 0, 1):
            i = source[n]
            remote(
                pk.at[mb, n], xin.at[mb, c, i], s_a.at[mb], r_a.at[mb, i], peer
            ).wait_recv()
            forward_copy(mb, n).start()
        own = remote(
            xin.at[mb, :, dp], xin.at[mb, :, zl * 2 + oc], s_o.at[mb], r_o.at[mb], peer
        )
        own.wait_recv()
        six = xin.at[mb, oc, 0:6]
        remote(six, six, s_f.at[mb], r_f.at[mb], peer).wait_recv()

    def project_in(mb, half):
        at = pl.ds(half * 2 * HQ, 2 * HQ)
        rows_in = jnp.concatenate([xin[mb, k].reshape(NDP * CAP, W) for k in range(2)], axis=1)
        total = jnp.dot(
            rows_in, wgu[:, :, at].reshape(2 * W, 2 * HQ), preferred_element_type=F32
        )
        part[mb, :, half] = total.reshape(NDP, CAP, 2 * HQ)

    def chain(d, k):
        half, u = rem(k, 2), div(k, 2)
        q, mb = rem(u, 4), div(u, 4)
        p = zl if d == 0 else 3 - zl
        up = (dp + 2 if d == 0 else dp - 2, ex)
        down = (dp - 2 if d == 0 else dp + 2, ex)
        slot = hid.at[u, c, half, 1 - d]
        own = part.at[mb, q + 4 * (1 - d), half]
        sums = remote(bsend.at[d, k], brecv.at[d, k], s_b.at[d], r_b.at[d, k], up)
        relay = remote(slot, slot, s_c.at[d], r_c.at[d, k], down)
        both = hid.at[u, c, :, 1 - d]
        across = remote(both, both, s_p.at[d], r_p.at[d, u], peer)
        return own, slot, p, sums, relay, across

    def chain_start(k):
        for d in range(2):

            @pl.when((zl if d == 0 else 3 - zl) == 0)
            def _():
                own, slot, p, sums, relay, across = chain(d, k)
                bsend[d, k] = own[...].astype(BF16)
                sums.start()

    def chain_step(t):
        for d in range(2):
            p0 = zl if d == 0 else 3 - zl
            k = t - SKEW * p0

            @pl.when((p0 > 0) & (k >= 0) & (k < NCH))
            def _():
                own, slot, p, sums, relay, across = chain(d, k)
                sums.wait_recv()

                @pl.when(p < 3)
                def _():
                    bsend[d, k] = (own[...] + brecv[d, k].astype(F32)).astype(BF16)
                    sums.start()

                @pl.when(p == 3)
                def _():
                    gate = own[:, 0:HQ] + brecv[d, k, :, 0:HQ].astype(F32)
                    lift = own[:, HQ : 2 * HQ] + brecv[d, k, :, HQ : 2 * HQ].astype(F32)
                    slot[...] = (gate / (1.0 + jnp.exp(-gate)) * lift).astype(BF16)
                    relay.start()

                    @pl.when(rem(k, 2) == 1)
                    def _():
                        across.start()

        for d in range(2):
            p0 = zl if d == 0 else 3 - zl
            k2 = t - 3 * SKEW - BACK * (3 - p0)

            @pl.when((p0 < 3) & (k2 >= 0) & (k2 < NCH))
            def _():
                own, slot, p, sums, relay, across = chain(d, k2)
                relay.wait_recv()

                @pl.when(p > 0)
                def _():
                    relay.start()

                @pl.when(rem(k2, 2) == 1)
                def _():
                    across.start()

    def chain_sends():
        for d in range(2):
            p = zl if d == 0 else 3 - zl
            sent = hid.at[:, c, :, 1 - d]

            @pl.when(p < 3)
            def _():
                remote(bsend.at[d], brecv.at[d], s_b.at[d], r_b.at[d, 0], peer).wait_send()

            @pl.when(p > 0)
            def _():
                remote(sent, sent, s_c.at[d], r_c.at[d, 0], peer).wait_send()

            remote(sent, sent, s_p.at[d], r_p.at[d, 0], peer).wait_send()

    def split(w):
        u, g = div(w, 2), rem(w, 2)
        return u, g, div(u, 4), rem(u, 4)

    def project_out(u):
        for g in range(2):
            there = hid.at[u, oc, :, g]
            remote(there, there, s_p.at[1 - g], r_p.at[1 - g, u], peer).wait_recv()
        parts = [hid[u, core, half].reshape(2 * CAP, HQ) for core in range(2) for half in range(2)]
        total = jnp.dot(
            jnp.concatenate(parts, axis=1), wd[...], preferred_element_type=F32
        )
        yv[...] = total.astype(BF16).reshape(2, CAP, W)

    to_x = [xdev(rem(x + a, 4)) for a in range(4)]
    to_y = [ydev(rem(y + a, 4)) for a in range(4)]

    def along(on_x, a):
        return (dp, jnp.where(on_x, to_x[a][1], to_y[a][1]))

    def e1_copy(w, a):
        g = rem(w, 2)
        to = rem(jnp.where(g == 0, x, y) + a, 4)
        return remote(e1s.at[w, to], e1r.at[w, a - 1], s_e1, r_e1.at[w], along(g == 0, a))

    def e2_copy(w, a):
        g = rem(w, 2)
        to = rem(jnp.where(g == 0, y, x) + a, 4)
        return remote(e2s.at[w, to], e2r.at[w, a - 1], s_e2, r_e2.at[w], along(g == 1, a))

    def spread(w):
        u, g, mb, q = split(w)

        @pl.when(g == 0)
        def _():
            project_out(u)

        spot = lax.broadcasted_iota(jnp.int32, (ROWS, CAP), 1).astype(F32)
        row = lax.broadcasted_iota(jnp.int32, (8, ROWS), 0)
        told = rtr[g * 4 + q]
        rank = jnp.sum(jnp.where(row == zh * 4 + mb, told, 0.0), axis=0, keepdims=True)
        share = jnp.sum(jnp.where(row == zh * 4 + 2 + mb, told, 0.0), axis=0, keepdims=True)
        turned = jnp.transpose(jnp.where(row == 0, rank, share))
        one = jnp.where(turned[:, 0:1] == spot, 1.0, 0.0).astype(BF16)
        value = turned[:, 1:2] * jnp.dot(one, yv[g], preferred_element_type=F32)
        value = value.reshape(4, 32, W)
        e1s[w] = value.astype(BF16)
        zf[...] = value
        for a in (2, 1, 3):
            e1_copy(w, a).start()
        zown[w] = zf[jnp.where(g == 0, x, y)]

    def combine1(w):
        remote(e1s.at[w, 0:3], e1r.at[w], s_e1, r_e1.at[w], peer).wait_recv()
        for d in range(2):
            rows = slice(16 * d, 16 * d + 16)
            total = zown[w, rows]
            for a in range(3):
                total = total + e1r[w, a, rows].astype(F32)
            for b in range(2):
                e2f[2 * d + b, 0:8] = total[8 * b : 8 * b + 8, 0:WF]
                e2f[2 * d + b, 8:16, 0 : W - WF] = total[8 * b : 8 * b + 8, WF:W]
        e2s[w] = e2f[...].astype(BF16)
        e2o[w] = e2f[jnp.where(rem(w, 2) == 0, y, x)]
        for a in (2, 1, 3):
            e2_copy(w, a).start()

    def deliver_copy(w, zz):
        u, g, mb, q = split(w)
        i = q + 4 * g
        dev = (i, (y * 2 + zz) * 4 + x)
        away = (i != dp) | (zh != zz)
        return away, remote(
            fs.at[w, zz], fr.at[mb, dp * 2 + zh], s_x, r_x.at[mb], dev
        )

    def combine2(w):
        u, g, mb, q = split(w)
        top = lax.broadcasted_iota(jnp.int32, (8, WF), 0) < 4
        remote(e2s.at[w, 0:3], e2r.at[w], s_e2, r_e2.at[w], peer).wait_recv()
        total = e2o[w]
        for a in range(3):
            total = total + e2r[w, a].astype(F32)
        lo, hi = total[0:8], total[8:16]
        fs[w, 0] = jnp.where(top, lo, pltpu.roll(hi, 4, 0))
        fs[w, 1] = jnp.where(top, pltpu.roll(lo, 4, 0), hi)
        for zz in range(2):
            away, cp = deliver_copy(w, zz)

            @pl.when(away)
            def _():
                cp.start()

            @pl.when(jnp.logical_not(away))
            def _():
                fr[mb, dp * 2 + zh] = fs[w, zz]

    def combine_sends():
        remote(e1s.at[:, 0:3], e1r, s_e1, r_e1.at[0], peer).wait_send()
        remote(e2s.at[:, 0:3], e2r, s_e2, r_e2.at[0], peer).wait_send()
        remote(fs.at[0:15], fs.at[0:15], s_x, r_x.at[0], peer).wait_send()

    def finish(mb):
        there = fr.at[mb, 0:15]
        remote(there, there, s_x, r_x.at[mb], peer).wait_recv()
        for j in range(NDP):
            total = (fr[mb, 2 * j] + fr[mb, 2 * j + 1]).astype(BF16)
            out_ref[mb, :, j * W : j * W + WF] = total[0:4]
            out_ref[mb, :, j * W + WF : (j + 1) * W] = total[4:8, 0 : W - WF]

    loads[0].wait()
    dispatch(0)
    for cp in weight_copies():
        cp.start()
    loads[1].wait()
    dispatch(1)
    announce()
    e2f[...] = jnp.zeros((4, 16, WF), F32)
    for k in range(4):
        loads[2 + k].wait()
    for k in range(4):
        ref, at = weight_at(k)
        remote(
            ref.at[0, :, hidden_at(oc, k // 2)], wgu.at[oc, :, at], s_w.at[k], r_w.at[k], peer
        ).wait_recv()
    collect(0)
    project_in(0, 0)
    chain_start(0)
    project_in(0, 1)

    @pl.loop(1, NCH // 2)
    def _(k):
        chain_start(k)

    for t in range(1, MID + 4):
        chain_step(t)
        if t == MID:
            collect(1)
        if t in (MID, MID + 2):
            project_in(1, (t - MID) // 2)

    @pl.loop(NCH // 2, NCH // 2 + AHEAD)
    def _(k):
        chain_start(k)

    loads[6].wait()
    tiles = remote(rtr.at[0:7], rtr.at[0:7], s_rt, r_rt, peer)
    tiles.wait_recv()

    tiles.wait_send()
    for cp in weight_copies():
        cp.wait_send()
    for mb in range(MB):
        own_copy(mb).wait_send()
        remote(pk.at[mb], pk.at[mb], s_a.at[mb], r_a.at[mb, 0], peer).wait_send()
        six = xin.at[mb, c, 0:6]
        remote(six, six, s_f.at[mb], r_f.at[mb], peer).wait_send()

    @pl.loop(MID + 4, PIECES + LAG2)
    def _(t):
        chain_step(t)

        @pl.when(t < NCH // 2 - AHEAD + MID + 4)
        def _():
            chain_start(t + NCH // 2 + AHEAD - MID - 4)

        @pl.when(t >= LAG2)
        def _():
            combine2(t - LAG2)

        @pl.when(t == PIECES + LAG2 - 1)
        def _():
            finish(0)

        @pl.when((t >= LAG1) & (t < LAG1 + PIECES))
        def _():
            combine1(t - LAG1)

        @pl.when((t >= LAG0) & (t < LAG0 + PIECES))
        def _():
            spread(t - LAG0)

    chain_sends()
    combine_sends()
    finish(1)


def per_device(tokens, scores, expert_ids, slot_expert, w_gate, w_up, w_down):
    vmem = pl.BlockSpec(memory_space=pltpu.VMEM)
    anywhere = pl.BlockSpec(memory_space=pl.ANY)
    dma = pltpu.SemaphoreType.DMA
    return pl.pallas_call(
        kernel,
        out_shape=jax.ShapeDtypeStruct((MB, 4, D), BF16),
        in_specs=[
            anywhere, vmem, vmem, pl.BlockSpec(memory_space=pltpu.SMEM),
            anywhere, anywhere, anywhere,
        ],
        out_specs=vmem,
        scratch_shapes=[
            pltpu.VMEM((MB, ROWS, D), BF16),
            pltpu.VMEM((2, W, H), BF16),
            pltpu.VMEM((H, W), BF16),
            pltpu.VMEM((2, MB, CAP, ROWS), BF16),
            pltpu.VMEM((MB, 6, CAP, W), BF16),
            pltpu.VMEM((MB, 2, NDP, CAP, W), BF16),
            pltpu.VMEM((MB, NDP, 2, CAP, 2 * HQ), F32),
            pltpu.VMEM((2, NCH, CAP, 2 * HQ), BF16),
            pltpu.VMEM((2, NCH, CAP, 2 * HQ), BF16),
            pltpu.VMEM((UNITS, 2, 2, 2, CAP, HQ), BF16),
            pltpu.VMEM((2, CAP, W), BF16),
            pltpu.VMEM((4, 32, W), F32),
            pltpu.VMEM((PIECES, 32, W), F32),
            pltpu.VMEM((PIECES, 4, 32, W), BF16),
            pltpu.VMEM((PIECES, 3, 32, W), BF16),
            pltpu.VMEM((4, 16, WF), F32),
            pltpu.VMEM((PIECES, 16, WF), F32),
            pltpu.VMEM((PIECES, 4, 16, WF), BF16),
            pltpu.VMEM((PIECES, 3, 16, WF), BF16),
            pltpu.VMEM((PIECES, 2, 8, WF), F32),
            pltpu.VMEM((MB, 2 * NDP, 8, WF), F32),
            pltpu.VMEM((8, ROWS), F32),
            pltpu.VMEM((NDP, 8, ROWS), F32),
            dma((7,)),
            dma((4,)), dma((4,)),
            dma, dma,
            dma((MB,)), dma((MB, NDP)),
            dma((MB,)), dma((MB,)),
            dma((MB,)), dma((MB,)),
            dma((2,)), dma((2, NCH)),
            dma((2,)), dma((2, NCH)),
            dma((2,)), dma((2, UNITS)),
            dma, dma((PIECES,)),
            dma, dma((PIECES,)),
            dma, dma((MB,)),
        ],
        compiler_params=pltpu.CompilerParams(
            collective_id=0, has_side_effects=True, vmem_limit_bytes=56 * 2**20
        ),
        name="expert_layer",
    )(
        tokens, jnp.swapaxes(scores, 1, 2), jnp.swapaxes(expert_ids, 1, 2), slot_expert,
        w_gate, w_up, w_down,
    )


def solution(mesh):
    in_specs = (
        P(None, "dp", None),
        P(None, "dp", None),
        P(None, "dp", None),
        P(),
        P("expert", "dp", None),
        P("expert", "dp", None),
        P("expert", None, "dp"),
    )
    out_specs = P(None, ("dp", "expert"), None)
    return jax.shard_map(
        per_device, mesh=mesh, in_specs=in_specs, out_specs=out_specs, check_vma=False
    )
```
